32 devices in a mesh: col: 4 (over z), depth: 8 (over y, x, core).
Axes of the slice: x: 2, y: 2, z: 4, core: 2. Of those that a mesh axis runs over, the one named last changes fastest.
Arguments:
- volume: bfloat16 [128, 256, 512], P('depth', None, 'col'), may hold values from -6 to 6
- tf_index: int32 [128, 256, 512], P('depth', None, 'col'), may hold values from 0 to 255
- tf_table: bfloat16 [4, 256], replicated, may hold values from 0 to 1, as said below
Outputs:
- frame: float32 [4, 256, 512], P(None, 'depth', 'col')
The draws below stay inside these ranges and needn't reach their ends.
Inputs may be any that keep to these rules, and one draw needn't show every extreme that they name: Rows 0 to 2 of tf_table are positive colours; row 3 is a positive extinction.
All inputs are finite; a program needn't handle non-finite values.
Results may differ from the reference program's by a relative error of at most 0.005.
Values may be sent and summed in bfloat16 or wider, within the bound.
A program may use at most 128 MiB of HBM per device.

```python
import math
import jax
import jax.numpy as jnp
from jax import lax

CY = 256
TABLE_ENTRIES = 256
NX = 512
NZ = 128


def draw_tf_table(key, part):
    color_random_key, extinction_random_key, threshold_random_key, surge_random_key = jax.random.split(key, 4)
    color_lo, color_hi, sigma_lo, sigma_hi = (0.2, 1.0, 0.2 / NZ, 4.0 / NZ)
    colors = jax.random.uniform(color_random_key, (3, TABLE_ENTRIES), jnp.float32, color_lo, color_hi)
    logs = jax.random.uniform(extinction_random_key, (TABLE_ENTRIES,), jnp.float32, math.log(sigma_lo), math.log(sigma_hi))
    extinction_coefficient = jnp.exp(logs)
    surge_threshold = jax.random.randint(threshold_random_key, (), 0, TABLE_ENTRIES)
    emission_surge = jax.random.uniform(surge_random_key, (), jnp.float32, 0.25, 0.5)
    extinction_coefficient = jnp.where(jnp.arange(TABLE_ENTRIES) == surge_threshold, emission_surge, extinction_coefficient)
    return jnp.concatenate([colors, extinction_coefficient[None]], 0).astype(jnp.bfloat16)


def set_ends(drawn, stream_key, smallest, largest):
    extent = drawn.shape
    index_at = [jax.random.randint(jax.random.fold_in(stream_key, axis), (), 0, extent[axis]) for axis in range(len(extent))]
    drawn = drawn.at[tuple(index_at)].set(smallest)
    longest = extent.index(max(extent))
    index_at[longest] = (index_at[longest] + 1) % extent[longest]
    return drawn.at[tuple(index_at)].set(largest)


def level_of(stream_key, extent, cuts, low, largest):
    factor_of = 1.0
    for position, parts in cuts:
        heights = jax.random.uniform(jax.random.fold_in(jax.random.fold_in(stream_key, 6), position), (parts,), jnp.float32, low / len(cuts), largest / len(cuts))
        factor_of = factor_of * jnp.repeat(jnp.exp(heights), extent[position] // parts).reshape((-1,) + (1,) * (len(extent) - 1 - position))
    return factor_of


def scatter_about(rng, shape, deviation, bound, shards=(), held_as=jnp.bfloat16):
    array = jax.random.normal(rng, shape, jnp.float32) * deviation
    if len(shards) > 0:
        array = level_of(rng, shape, shards, -0.22, 0.18) * array
    return jnp.clip(array, min=-bound, max=bound).astype(held_as)


def setup_inputs(seed: int = 0) -> dict:
    streams_of = jax.random.split(jax.random.key(seed), 4)
    return {
        "volume": scatter_about(streams_of[0], (NZ, CY, NX), 1.0, 6.0, ((0, 8), (2, 4))),
        "tf_index": set_ends(jax.random.randint(streams_of[1], (NZ, CY, NX), 0, TABLE_ENTRIES), jax.random.fold_in(streams_of[1], 1), 0, TABLE_ENTRIES - 1).astype(jnp.int32),
        "tf_table": draw_tf_table(jax.random.fold_in(streams_of[3], 71), 0),
    }


light_across = 0.36
light_down = 0.48
light_depth = 0.8

def shading(grad_x, grad_y, grad_z):
    facing = grad_x * light_across + grad_y * light_down + grad_z * light_depth
    return 0.25 + 0.75 * jnp.abs(facing) / jnp.sqrt(grad_x * grad_x + grad_y * grad_y + grad_z * grad_z + 1.0)

def reference(volume, tf_index, tf_table):
    padded = jnp.pad(volume, ((1, 1), (1, 1), (1, 1)))
    table = tf_table.astype(jnp.float32)

    def march(carry, depth_pos):
        color_sum, optical = carry
        above = lax.dynamic_index_in_dim(padded, depth_pos, 0, keepdims=False).astype(jnp.float32)
        middle = lax.dynamic_index_in_dim(padded, depth_pos + 1, 0, keepdims=False).astype(jnp.float32)
        below = lax.dynamic_index_in_dim(padded, depth_pos + 2, 0, keepdims=False).astype(jnp.float32)
        grad_x = (middle[1:-1, 2:] - middle[1:-1, :-2]) * 0.5
        grad_y = (middle[2:, 1:-1] - middle[:-2, 1:-1]) * 0.5
        grad_z = (below[1:-1, 1:-1] - above[1:-1, 1:-1]) * 0.5
        shade = shading(grad_x, grad_y, grad_z)
        levels = lax.dynamic_index_in_dim(tf_index, depth_pos, 0, keepdims=False)
        looked = table[:, levels]
        extinction_coefficient = looked[3]
        alpha = -jnp.expm1(-extinction_coefficient)
        weight = jnp.exp(-optical) * alpha * shade
        color_sum = color_sum + weight[None] * looked[:3]
        return ((color_sum, optical + extinction_coefficient), None)
    start = (jnp.zeros((3, CY, NX), jnp.float32), jnp.zeros((CY, NX), jnp.float32))
    (color_sum, optical), _ = lax.scan(march, start, jnp.arange(NZ, dtype=jnp.int32))
    return jnp.concatenate([color_sum, (-jnp.expm1(-optical))[None]], 0)
```

```python
import functools

import jax
import jax.numpy as jnp
from jax import lax
from jax.experimental import pallas as pl
from jax.experimental.pallas import tpu as pltpu
from jax.sharding import PartitionSpec as P

LIGHT = (0.75 * 0.36, 0.75 * 0.48, 0.75 * 0.8)
LOG2E = 1.4426950408889634
LN2 = 0.6931471805599453
PAD = 8


def one_minus_exp(x):
    series = x * (1.0 - x * (0.5 - x * (1.0 / 6.0 - x * (1.0 / 24.0 - x * (1.0 / 120.0)))))
    return jnp.where(x < 0.125, series, 1.0 - jnp.exp(-x))


def kernel(n, m, vol_hbm, idx_hbm, table_hbm, out, vol, idx, table, load_sem, pre, fvol, dx, part, recv, edge, zlo, zhi, from_left, from_right,
           send_sem, recv_sem, halo_send, halo_recv):
    depth, rows, cols = vol.shape
    rb = rows // n
    me = lax.axis_index("depth")
    mine = lax.axis_index("col")

    loads = [pltpu.make_async_copy(src, dst, load_sem.at[i]) for i, (src, dst) in
             enumerate(((table_hbm, table), (vol_hbm, vol), (idx_hbm, idx)))]
    for load in loads:
        load.start()

    barrier = pltpu.get_barrier_semaphore()

    def greet(k, c):
        pl.semaphore_signal(barrier, inc=1, device_id={"depth": lax.rem(me + 1 + k, n)},
                            device_id_type=pl.DeviceIdType.MESH)
        return c

    lax.fori_loop(0, n - 1, greet, 0)
    for there, side in ((mine > 0, -1), (mine < m - 1, 1)):
        @pl.when(there)
        def _():
            pl.semaphore_signal(barrier, inc=1, device_id={"col": mine + side},
                                device_id_type=pl.DeviceIdType.MESH)

    def halo_copy(k, src, dst, axis, to):
        return pltpu.make_async_remote_copy(
            src_ref=src, dst_ref=dst, send_sem=halo_send.at[k], recv_sem=halo_recv.at[k],
            device_id={axis: to}, device_id_type=pl.DeviceIdType.MESH)

    along_z = ((me > 0, me < n - 1, halo_copy(0, vol.at[0], zhi, "depth", me - 1), zhi),
               (me < n - 1, me > 0, halo_copy(1, vol.at[depth - 1], zlo, "depth", me + 1), zlo))
    along_x = ((mine > 0, mine < m - 1, halo_copy(2, edge, from_right, "col", mine - 1), from_right),
               (mine < m - 1, mine > 0, halo_copy(3, edge, from_left, "col", mine + 1), from_left))

    def send(halos):
        for sends, _, copy, _ in halos:
            pl.when(sends)(copy.start)

    def receive(halos):
        for sends, receives, copy, landed in halos:
            pl.when(sends)(copy.wait_send)
            pl.when(receives)(copy.wait_recv)

            @pl.when(jnp.logical_not(receives))
            def _():
                landed[...] = jnp.zeros_like(landed)

    loads[1].wait()
    r_i = lax.broadcasted_iota(jnp.int32, (cols, cols), 0)
    c_i = lax.broadcasted_iota(jnp.int32, (cols, cols), 1)
    diff = jnp.where(r_i == c_i + 1, 1.0, 0.0) - jnp.where(r_i == c_i - 1, 1.0, 0.0)
    diff = diff.astype(jnp.bfloat16)
    zero = jnp.zeros((PAD, cols), jnp.float32)

    def pick(z, total):
        at = jnp.where((r_i == cols - 1) & (c_i == z), 1.0, 0.0)
        at = at + jnp.where((r_i == 0) & (c_i == depth + z), 1.0, 0.0)
        return total + jnp.dot(vol[z], at.astype(jnp.bfloat16), preferred_element_type=jnp.float32)

    edges = lax.fori_loop(0, depth, pick, jnp.zeros((rows, cols), jnp.float32), unroll=True)
    fold = cols // (2 * depth)
    short = rows // fold
    packed = edges[:short]
    for i in range(1, fold):
        packed = packed + pltpu.roll(edges[i * short:(i + 1) * short], 2 * depth * i, 1)
    edge[...] = packed.astype(jnp.bfloat16)
    neighbours = (mine > 0).astype(jnp.int32) + (mine < m - 1).astype(jnp.int32)
    pl.semaphore_wait(barrier, n - 1 + neighbours)
    send(along_z)

    send(along_x)

    loads[0].wait()
    entries = table[...].astype(jnp.float32)
    sigma = entries[3:4]
    alpha = one_minus_exp(sigma)
    logs = [jnp.log(jnp.maximum(v, 1.2e-38)) * LOG2E
            for v in [entries[c:c + 1] * alpha for c in range(3)] + [sigma * LOG2E]]
    most = [jnp.max(v, axis=1, keepdims=True) for v in logs]
    least = [jnp.min(v, axis=1, keepdims=True) for v in logs]
    middle = [0.5 * (a + b) for a, b in zip(most, least)]
    grain = [jnp.maximum(a - b, 1e-3) * (1.0 / 65532.0) for a, b in zip(most, least)]
    place = [(v - o) / g for v, o, g in zip(logs, middle, grain)]

    def word(upper, lower):
        lower = jnp.floor(lower + 0.5)
        upper = jnp.floor(upper - lower * (1.0 / 65536.0) + 0.5)
        return upper.astype(jnp.int32) * 65536 + lower.astype(jnp.int32)

    sub = 8
    words = (word(place[0], place[1]), word(place[2], place[3]))
    low = [jnp.broadcast_to(t[:, :128], (sub, 128)) for t in words]
    high = [jnp.broadcast_to(t[:, 128:], (sub, 128)) for t in words]
    spread = [jnp.broadcast_to(g * (1.0 / 65536.0), (sub, cols)) for g in grain]
    sigma_middle = jnp.broadcast_to(middle[3], (sub, cols))
    scale = [jnp.broadcast_to(jnp.exp2(o), (sub, cols)) for o in middle[:3]]

    def search(word, z, r0):
        label = idx[z, pl.ds(r0, sub)]
        lane = label & 127
        return jnp.where(label < 128, jnp.take_along_axis(low[word], lane, axis=1),
                         jnp.take_along_axis(high[word], lane, axis=1))

    loads[2].wait()

    early = depth * 12 // 16

    def widen(z, c):
        def rows_of(i, c):
            r0 = pl.multiple_of(i * sub, sub)
            pre[z, pl.ds(r0, sub)] = search(0, z, r0)
            return c

        @pl.when(z < early)
        def _():
            lax.fori_loop(0, rows // sub, rows_of, 0, unroll=True)

        v = vol[z]
        fvol[z + 1, :PAD] = zero
        fvol[z + 1, PAD + rows:] = zero
        fvol[z + 1, PAD:PAD + rows] = v.astype(jnp.float32)
        return c

    lax.fori_loop(0, depth, widen, 0)
    receive(along_x)
    lane = lax.broadcasted_iota(jnp.int32, (short, cols), 1)
    packed = jnp.where(lax.rem(lane, 2 * depth) < depth, from_left[...].astype(jnp.float32),
                       from_right[...].astype(jnp.float32))
    halo = [packed] + [pltpu.roll(packed, cols - 2 * depth * i, 1) for i in range(1, fold)]
    halo = jnp.concatenate(halo, 0).astype(jnp.bfloat16)

    def stage(z, c):
        v = vol[z]
        ends = jnp.where((c_i == cols - 1) & (r_i == depth + z), 1.0, 0.0)
        ends = ends - jnp.where((c_i == 0) & (r_i == z), 1.0, 0.0)
        weights = jnp.concatenate([diff, ends.astype(jnp.bfloat16)], 0)
        both = jnp.concatenate([v, halo], 1)
        dx[z] = jnp.dot(both, weights, preferred_element_type=jnp.float32)
        return c

    lax.fori_loop(0, depth, stage, 0, unroll=8)
    receive(along_z)
    fvol[0, PAD:PAD + rows] = zlo[...].astype(jnp.float32)
    fvol[depth + 1, PAD:PAD + rows] = zhi[...].astype(jnp.float32)

    def block(r0):
        def step(z, carry, known):
            acc0, acc1, acc2, s = carry
            at = pl.multiple_of(PAD + r0, 8)
            gx = dx[z, pl.ds(pl.multiple_of(r0, 8), sub)]
            gy = fvol[z + 1, pl.ds(at + 1, sub)] - fvol[z + 1, pl.ds(at - 1, sub)]
            gz = fvol[z + 2, pl.ds(at, sub)] - fvol[z, pl.ds(at, sub)]
            facing = gx * LIGHT[0] + gy * LIGHT[1] + gz * LIGHT[2]
            inv = lax.rsqrt(gx * gx + gy * gy + (gz * gz + 4.0))
            shade = 0.25 + jnp.abs(facing) * inv
            r1 = pl.multiple_of(r0, 8)
            first = pre[z, pl.ds(r1, sub)] if known else search(0, z, r1)
            second = search(1, z, r1)
            codes = (first, first << 16, second, second << 16)
            code0, code1, code2, code3 = [c.astype(jnp.float32) * g for c, g in zip(codes, spread)]
            return (acc0 + jnp.exp2(code0 + s) * shade, acc1 + jnp.exp2(code1 + s) * shade,
                    acc2 + jnp.exp2(code2 + s) * shade, s - jnp.exp2(code3 + sigma_middle))

        init = tuple(jnp.zeros((sub, cols), jnp.float32) for _ in range(4))
        sums = lax.fori_loop(0, early, functools.partial(step, known=True), init, unroll=True)
        sums = lax.fori_loop(early, depth, functools.partial(step, known=False), sums, unroll=True)
        return tuple(a * g for a, g in zip(sums[:3], scale)) + sums[3:]

    def compute(d):
        tiles = [block(d * rb + sub * i) for i in range(rb // sub)]
        return jnp.concatenate([t[c] for c in range(4) for t in tiles], 0).astype(jnp.bfloat16)

    def copy(k):
        return pltpu.make_async_remote_copy(
            src_ref=part.at[k], dst_ref=recv.at[k],
            send_sem=send_sem.at[k], recv_sem=recv_sem.at[k],
            device_id={"depth": lax.rem(me + 1 + k, n)},
            device_id_type=pl.DeviceIdType.MESH)

    def work(k, c):
        part[k] = compute(lax.rem(me + 1 + k, n))
        copy(k).start()
        return c

    lax.fori_loop(0, n - 1, work, 0)
    recv[n - 1] = compute(me)

    def arrive(k, c):
        copy(k).wait()
        return c

    lax.fori_loop(0, n - 1, arrive, 0)

    def over(j, carry):
        color, s = carry
        piece = recv[lax.rem(me - j - 1 + 2 * n, n)].astype(jnp.float32)
        t = jnp.exp2(s)
        color = tuple(color[c] + t * piece[c * rb:(c + 1) * rb] for c in range(3))
        return color, s + piece[3 * rb:]

    init = jnp.zeros((rb, cols), jnp.float32)
    color, s = lax.fori_loop(0, n, over, ((init,) * 3, init))
    for c in range(3):
        out[c] = color[c]
    out[3] = one_minus_exp(s * -LN2)


def on_device(volume, tf_index, tf_table):
    depth, rows, cols = volume.shape
    n = lax.axis_size("depth")
    m = lax.axis_size("col")
    vm = pl.BlockSpec(memory_space=pltpu.VMEM)
    rb = rows // n
    return pl.pallas_call(
        functools.partial(kernel, n, m),
        out_shape=jax.ShapeDtypeStruct((4, rb, cols), jnp.float32),
        in_specs=[pl.BlockSpec(memory_space=pltpu.HBM)] * 3,
        out_specs=vm,
        scratch_shapes=[
            pltpu.VMEM(volume.shape, volume.dtype),
            pltpu.VMEM(tf_index.shape, tf_index.dtype),
            pltpu.VMEM(tf_table.shape, tf_table.dtype),
            pltpu.SemaphoreType.DMA((3,)),
            pltpu.VMEM(tf_index.shape, jnp.int32),
            pltpu.VMEM((depth + 2, rows + 2 * PAD, cols), jnp.float32),
            pltpu.VMEM((depth, rows, cols), jnp.float32),
            pltpu.VMEM((n, 4 * rb, cols), jnp.bfloat16),
            pltpu.VMEM((n, 4 * rb, cols), jnp.bfloat16),
            pltpu.VMEM((2 * rows * depth // cols, cols), jnp.bfloat16),
            *[pltpu.VMEM((rows, cols), jnp.bfloat16)] * 2,
            *[pltpu.VMEM((2 * rows * depth // cols, cols), jnp.bfloat16)] * 2,
            pltpu.SemaphoreType.DMA((n - 1,)),
            pltpu.SemaphoreType.DMA((n - 1,)),
            pltpu.SemaphoreType.DMA((4,)),
            pltpu.SemaphoreType.DMA((4,)),
        ],
        compiler_params=pltpu.CompilerParams(
            collective_id=0, has_side_effects=True, vmem_limit_bytes=53 * 1024 * 1024),
    )(volume, tf_index, tf_table)


def solution(mesh):
    in_specs = (P("depth", None, "col"), P("depth", None, "col"), P())
    out_specs = P(None, "depth", "col")
    return jax.shard_map(
        on_device, mesh=mesh, in_specs=in_specs, out_specs=out_specs, check_vma=False
    )
```

```python
import functools

import jax
import jax.numpy as jnp
from jax import lax
from jax.experimental import pallas as pl
from jax.experimental.pallas import tpu as pltpu
from jax.sharding import PartitionSpec as P

LIGHT = (0.75 * 0.36, 0.75 * 0.48, 0.75 * 0.8)
LOG2E = 1.4426950408889634
LN2 = 0.6931471805599453
PAD = 8
SUB = 8
UNIT = 32
MESH = pl.DeviceIdType.MESH


def one_minus_exp(x):
    series = x * (1.0 - x * (0.5 - x * (1.0 / 6.0 - x * (1.0 / 24.0 - x * (1.0 / 120.0)))))
    return jnp.where(x < 0.125, series, 1.0 - jnp.exp(-x))


def place_of(k, mine, count):
    if count & (count - 1):
        return lax.rem(mine + 1 + k, count)
    mask, out = count - 1 - k, 0
    for i in range(count.bit_length() - 1):
        out = out + lax.rem(lax.div(mine, 1 << i) + lax.div(mask, 1 << i), 2) * (1 << i)
    return out


def take(row, lane):
    return jnp.take_along_axis(row, lane, axis=1, mode="promise_in_bounds")


def kernel(n, m, vol_hbm, idx_hbm, table_hbm, out, vol, idx, table, load_sem, fvol, weight, across, slope, square, base, depths,
           part, recv, edge, zlo, zhi, from_left, from_right, halo, send_sem, recv_sem, halo_send, halo_recv):
    depth, rows, cols = vol.shape
    rb = rows // n
    group = UNIT // rb
    units = rows // UNIT
    tiles = UNIT // SUB
    me = lax.axis_index("depth")
    mine = lax.axis_index("col")
    my_unit = lax.div(me, group)

    def load_labels(k):
        at = pl.ds(pl.multiple_of(place_of(k, my_unit, units) * UNIT, UNIT), UNIT)
        return pltpu.make_async_copy(idx_hbm.at[:, at], idx.at[:, at], load_sem.at[2 + k])

    loads = [pltpu.make_async_copy(src, dst, load_sem.at[i]) for i, (src, dst) in
             enumerate(((table_hbm, table), (vol_hbm, vol)))]
    for load in loads:
        load.start()
    lax.fori_loop(0, units, lambda k, c: (load_labels(k).start(), c)[1], 0)

    barrier = pltpu.get_barrier_semaphore()

    def greet(k, c):
        pl.semaphore_signal(barrier, inc=1, device_id={"depth": lax.rem(me + 1 + k, n)}, device_id_type=MESH)
        return c

    lax.fori_loop(0, n - 1, greet, 0)
    for there, side in ((mine > 0, -1), (mine < m - 1, 1)):
        @pl.when(there)
        def _():
            pl.semaphore_signal(barrier, inc=1, device_id={"col": mine + side}, device_id_type=MESH)

    def halo_copy(k, src, dst, axis, to):
        return pltpu.make_async_remote_copy(
            src_ref=src, dst_ref=dst, send_sem=halo_send.at[k], recv_sem=halo_recv.at[k],
            device_id={axis: to}, device_id_type=MESH)

    halos = ((mine > 0, mine < m - 1, halo_copy(2, edge, from_right, "col", mine - 1), from_right),
             (mine < m - 1, mine > 0, halo_copy(3, edge, from_left, "col", mine + 1), from_left),
             (me > 0, me < n - 1, halo_copy(0, vol.at[0], zhi, "depth", me - 1), zhi),
             (me < n - 1, me > 0, halo_copy(1, vol.at[depth - 1], zlo, "depth", me + 1), zlo))

    r_i = lax.broadcasted_iota(jnp.int32, (cols, cols), 0)
    c_i = lax.broadcasted_iota(jnp.int32, (cols, cols), 1)
    diff = jnp.where(r_i == c_i + 1, 1.0, 0.0) - jnp.where(r_i == c_i - 1, 1.0, 0.0)
    diff = diff.astype(jnp.bfloat16)
    zero = jnp.zeros((PAD, cols), jnp.float32)

    loads[0].wait()
    entries = table[...].astype(jnp.float32)
    sigma = entries[3:4]
    alpha = one_minus_exp(sigma)
    logs = [jnp.log(jnp.maximum(v, 1.2e-38)) * LOG2E
            for v in [entries[c:c + 1] * alpha for c in range(3)] + [sigma * LOG2E]]
    most = [jnp.max(v, axis=1, keepdims=True) for v in logs]
    least = [jnp.min(v, axis=1, keepdims=True) for v in logs]
    middle = [0.5 * (a + b) for a, b in zip(most, least)]
    grain = [jnp.maximum(a - b, 1e-3) * (1.0 / 65532.0) for a, b in zip(most, least)]
    place = [(v - o) / g for v, o, g in zip(logs, middle, grain)]

    def word(upper, lower):
        lower = jnp.floor(lower + 0.5)
        upper = jnp.floor(upper - lower * (1.0 / 65536.0) + 0.5)
        return upper.astype(jnp.int32) * 65536 + lower.astype(jnp.int32)

    words = (word(place[0], place[1]), word(place[2], place[3]))
    low = [jnp.broadcast_to(t[:, :128], (SUB, 128)) for t in words]
    high = [jnp.broadcast_to(t[:, 128:], (SUB, 128)) for t in words]
    spread = [jnp.broadcast_to(g * (1.0 / 65536.0), (SUB, cols)) for g in grain]
    sigma_middle = jnp.broadcast_to(middle[3], (SUB, cols))
    scale = [jnp.broadcast_to(jnp.exp2(o), (SUB, cols)) for o in middle[:3]]

    loads[1].wait()

    def pick(z, total):
        at = jnp.where((r_i == cols - 1) & (c_i == z), 1.0, 0.0)
        at = at + jnp.where((r_i == 0) & (c_i == depth + z), 1.0, 0.0)
        return total + jnp.dot(vol[z], at.astype(jnp.bfloat16), preferred_element_type=jnp.float32)

    edges = lax.fori_loop(0, depth, pick, jnp.zeros((rows, cols), jnp.float32), unroll=True)
    edge[...] = edges.astype(jnp.bfloat16)

    def widen(z, c):
        fvol[z + 1, :PAD] = zero
        fvol[z + 1, PAD + rows:] = zero
        fvol[z + 1, PAD:PAD + rows] = vol[z].astype(jnp.float32)
        return c

    lax.fori_loop(0, depth, widen, 0)

    def look(k, c):
        @pl.when(k == 1)
        def _():
            neighbours = (mine > 0).astype(jnp.int32) + (mine < m - 1).astype(jnp.int32)
            pl.semaphore_wait(barrier, n - 1 + neighbours)
            for sends, _, copy, _ in halos:
                pl.when(sends)(copy.start)

        load_labels(k).wait()
        u0 = pl.multiple_of(place_of(k, my_unit, units) * UNIT, UNIT)
        sums = [[jnp.zeros((SUB, cols), jnp.float32) for _ in range(4)] for _ in range(tiles)]
        def decode(z, i, first, second, gxs):
            r = slice(i * SUB, (i + 1) * SUB)
            acc0, acc1, acc2, s = sums[i]
            codes = (first, first << 16, second, second << 16)
            code0, code1, code2, code3 = [v.astype(jnp.float32) * g for v, g in zip(codes, spread)]
            w0, w1, w2 = jnp.exp2(code0 + s), jnp.exp2(code1 + s), jnp.exp2(code2 + s)
            weight[k, 0, z, r], weight[k, 1, z, r], weight[k, 2, z, r] = w0, w1, w2
            sums[i] = [acc0 + w0, acc1 + w1, acc2 + w2, s - jnp.exp2(code3 + sigma_middle)]
            at = pl.multiple_of(PAD + u0 + i * SUB, SUB)
            gy = fvol[z + 1, pl.ds(at + 1, SUB)] - fvol[z + 1, pl.ds(at - 1, SUB)]
            facing = gy * LIGHT[1]
            norm = gy * gy + 4.0
            if 0 < z < depth - 1:
                gz = fvol[z + 2, pl.ds(at, SUB)] - fvol[z, pl.ds(at, SUB)]
                facing = facing + gz * LIGHT[2]
                norm = norm + gz * gz
            across[k, z, r] = gxs[r]
            slope[k, z, r] = facing
            square[k, z, r] = norm

        places = [(z, i) for z in range(depth) for i in range(tiles)]
        gx = [jnp.dot(vol[z, pl.ds(u0, UNIT)], diff, preferred_element_type=jnp.float32) for z in range(depth)]
        got, busy, open_at = {}, [3, 0], [None, None]
        fresh = iter(places)
        decoded = 0
        while decoded < len(places):
            side = 1 if busy[1] <= busy[0] else 0
            if open_at[side] is None:
                place = next(fresh, None)
                if place is None:
                    side = 1 - side
                    if open_at[side] is None:
                        break
                else:
                    z, i = place
                    label = idx[z, pl.ds(u0 + i * SUB, SUB)]
                    open_at[side] = (place, label & 127, label < 128, [])
                    busy[side] += 1 - side
            place, lane, lower, words = open_at[side]
            words.append(take((low[1], high[1], low[0], high[0])[len(words)], lane))
            busy[side] += 1
            if len(words) == 4:
                got[place] = jnp.where(lower, words[2], words[3]), jnp.where(lower, words[0], words[1])
                open_at[side] = None
            while decoded < len(places) and places[decoded] in got:
                z, i = places[decoded]
                decode(z, i, *got[z, i], gx[z])
                decoded += 1
        for i in range(tiles):
            r = slice(i * SUB, (i + 1) * SUB)
            for c3 in range(3):
                base[k, c3, r] = sums[i][c3] * 0.25
            depths[k, r] = sums[i][3]
        return c

    lax.fori_loop(0, units, look, 0)

    for sends, receives, copy, landed in halos:
        pl.when(sends)(copy.wait_send)
        pl.when(receives)(copy.wait_recv)

        @pl.when(jnp.logical_not(receives))
        def _():
            landed[...] = jnp.zeros_like(landed)

    fvol[0, PAD:PAD + rows] = zlo[...].astype(jnp.float32)
    fvol[depth + 1, PAD:PAD + rows] = zhi[...].astype(jnp.float32)
    lane = lax.broadcasted_iota(jnp.int32, (rows, cols), 1)
    halo[...] = jnp.where(lane < depth, -from_left[...].astype(jnp.float32),
                          jnp.where(lane < 2 * depth, from_right[...].astype(jnp.float32), 0.0))
    lane = lax.broadcasted_iota(jnp.int32, (SUB, cols), 1)

    def copy(k, j):
        to = place_of(k, my_unit, units) * group + j
        return to, pltpu.make_async_remote_copy(
            src_ref=part.at[k, j], dst_ref=recv.at[me], send_sem=send_sem.at[k, j], recv_sem=recv_sem.at[me],
            device_id={"depth": to}, device_id_type=MESH)

    def shade(k, c):
        u0 = pl.multiple_of(place_of(k, my_unit, units) * UNIT, UNIT)
        sums = [[base[k, c3, i * SUB:(i + 1) * SUB] for c3 in range(3)] for i in range(tiles)]
        ends = [halo[pl.ds(u0 + i * SUB, SUB)] for i in range(tiles)]
        for z in range(depth):
            outer = jnp.where(lane == 0, z, jnp.where(lane == cols - 1, depth + z, cols - 1))
            for i in range(tiles):
                r = slice(i * SUB, (i + 1) * SUB)
                gx = across[k, z, r] + take(ends[i], outer)
                facing = slope[k, z, r] + gx * LIGHT[0]
                norm = square[k, z, r] + gx * gx
                if z == 0 or z == depth - 1:
                    at = pl.multiple_of(PAD + u0 + i * SUB, SUB)
                    gz = fvol[z + 2, pl.ds(at, SUB)] - fvol[z, pl.ds(at, SUB)]
                    facing = facing + gz * LIGHT[2]
                    norm = norm + gz * gz
                lit = jnp.abs(facing) * lax.rsqrt(norm)
                sums[i] = [a + weight[k, c3, z, r] * lit for c3, a in enumerate(sums[i])]
        color = [jnp.concatenate([sums[i][c3] * scale[c3] for i in range(tiles)], 0) for c3 in range(3)]
        color.append(depths[k])
        for j in range(group):
            part[k, j] = jnp.concatenate([v[j * rb:(j + 1) * rb] for v in color], 0).astype(jnp.bfloat16)
            to, send = copy(k, j)
            pl.when(to != me)(send.start)
        return c

    lax.fori_loop(0, units, shade, 0)
    recv[me] = part[units - 1, lax.rem(me, group)]

    def arrive(k, c):
        @pl.when(k != me)
        def _():
            pltpu.make_async_remote_copy(
                src_ref=part.at[0, 0], dst_ref=recv.at[k], send_sem=send_sem.at[0, 0], recv_sem=recv_sem.at[k],
                device_id={"depth": k}, device_id_type=MESH).wait_recv()
        return c

    lax.fori_loop(0, n, arrive, 0)

    def over(j, carry):
        color, s = carry
        piece = recv[j].astype(jnp.float32)
        t = jnp.exp2(s)
        color = tuple(color[c] + t * piece[c * rb:(c + 1) * rb] for c in range(3))
        return color, s + piece[3 * rb:]

    init = jnp.zeros((rb, cols), jnp.float32)
    color, s = lax.fori_loop(0, n, over, ((init,) * 3, init), unroll=8)
    for c in range(3):
        out[c] = color[c]
    out[3] = one_minus_exp(s * -LN2)

    def left(k, c):
        for j in range(group):
            to, send = copy(k, j)
            pl.when(to != me)(send.wait_send)
        return c

    lax.fori_loop(0, units, left, 0)


def on_device(volume, tf_index, tf_table):
    depth, rows, cols = volume.shape
    n = lax.axis_size("depth")
    m = lax.axis_size("col")
    vm = pl.BlockSpec(memory_space=pltpu.VMEM)
    rb = rows // n
    units, group = rows // UNIT, UNIT // rb
    return pl.pallas_call(
        functools.partial(kernel, n, m),
        out_shape=jax.ShapeDtypeStruct((4, rb, cols), jnp.float32),
        in_specs=[pl.BlockSpec(memory_space=pltpu.HBM)] * 3,
        out_specs=vm,
        scratch_shapes=[
            pltpu.VMEM(volume.shape, volume.dtype),
            pltpu.VMEM(tf_index.shape, tf_index.dtype),
            pltpu.VMEM(tf_table.shape, tf_table.dtype),
            pltpu.SemaphoreType.DMA((2 + units,)),
            pltpu.VMEM((depth + 2, rows + 2 * PAD, cols), jnp.float32),
            pltpu.VMEM((units, 3, depth, UNIT, cols), jnp.float32),
            *[pltpu.VMEM((units, depth, UNIT, cols), jnp.float32)] * 3,
            pltpu.VMEM((units, 3, UNIT, cols), jnp.float32),
            pltpu.VMEM((units, UNIT, cols), jnp.float32),
            pltpu.VMEM((units, group, 4 * rb, cols), jnp.bfloat16),
            pltpu.VMEM((n, 4 * rb, cols), jnp.bfloat16),
            *[pltpu.VMEM((rows, cols), jnp.bfloat16)] * 5,
            pltpu.VMEM((rows, cols), jnp.float32),
            pltpu.SemaphoreType.DMA((units, group)),
            pltpu.SemaphoreType.DMA((n,)),
            pltpu.SemaphoreType.DMA((4,)),
            pltpu.SemaphoreType.DMA((4,)),
        ],
        compiler_params=pltpu.CompilerParams(
            collective_id=0, has_side_effects=True, vmem_limit_bytes=53 * 1024 * 1024),
    )(volume, tf_index, tf_table)


def solution(mesh):
    in_specs = (P("depth", None, "col"), P("depth", None, "col"), P())
    out_specs = P(None, "depth", "col")
    return jax.shard_map(
        on_device, mesh=mesh, in_specs=in_specs, out_specs=out_specs, check_vma=False
    )
```

```python
import functools

import jax
import jax.numpy as jnp
from jax import lax
from jax.experimental import pallas as pl
from jax.experimental.pallas import tpu as pltpu
from jax.sharding import PartitionSpec as P

LIGHT = (0.75 * 0.36, 0.75 * 0.48, 0.75 * 0.8)
LOG2E = 1.4426950408889634
LN2 = 0.6931471805599453
PAD = 8
SUB = 8
UNIT = 32
CHUNKS = 4
MESH = pl.DeviceIdType.MESH


def one_minus_exp(x):
    series = x * (1.0 - x * (0.5 - x * (1.0 / 6.0 - x * (1.0 / 24.0 - x * (1.0 / 120.0)))))
    return jnp.where(x < 0.125, series, 1.0 - jnp.exp(-x))


def place_of(k, mine, count):
    if count & (count - 1):
        return lax.rem(mine + 1 + k, count)
    half = count // 2
    mask, out = jnp.where(k < half, count - 1 - 2 * k, 2 * (count - 1 - k)), 0
    for i in range(count.bit_length() - 1):
        out = out + lax.rem(lax.div(mine, 1 << i) + lax.div(mask, 1 << i), 2) * (1 << i)
    return out


def take(row, lane):
    return jnp.take_along_axis(row, lane, axis=1, mode="promise_in_bounds")


def kernel(n, m, vol_hbm, idx_hbm, table_hbm, out, vol, idx, table, load_sem, fvol, weight, across, slope, square, base, depths,
           part, other, mix, recv, edge, from_left, from_right, zlo, zhi, halo, pair_send, pair_recv, send_sem, recv_sem, halo_send, halo_recv):
    depth, rows, cols = vol.shape
    rb = rows // n
    group = UNIT // rb
    units = rows // UNIT
    tiles = UNIT // SUB
    me = lax.axis_index("depth")
    mine = lax.axis_index("col")
    my_unit = lax.div(me, group)

    def load_labels(k):
        at = pl.ds(pl.multiple_of(place_of(k, my_unit, units) * UNIT, UNIT), UNIT)
        return pltpu.make_async_copy(idx_hbm.at[:, at], idx.at[:, at], load_sem.at[k])

    step = depth // CHUNKS
    loads = [pltpu.make_async_copy(table_hbm, table, load_sem.at[units])]
    for i in range(CHUNKS):
        at = pl.ds(i * step, step)
        loads.append(pltpu.make_async_copy(vol_hbm.at[at], vol.at[at], load_sem.at[units + 1 + i]))
    for load in loads:
        load.start()
    lax.fori_loop(0, units, lambda k, c: (load_labels(k).start(), c)[1], 0)

    barrier = pltpu.get_barrier_semaphore()

    def greet(k, c):
        pl.semaphore_signal(barrier, inc=1, device_id={"depth": lax.rem(me + 1 + k, n)}, device_id_type=MESH)
        return c

    lax.fori_loop(0, n - 1, greet, 0)
    for there, side in ((mine > 0, -1), (mine < m - 1, 1)):
        @pl.when(there)
        def _():
            pl.semaphore_signal(barrier, inc=1, device_id={"col": mine + side}, device_id_type=MESH)

    def halo_copy(k, src, dst, axis, to):
        return pltpu.make_async_remote_copy(
            src_ref=src, dst_ref=dst, send_sem=halo_send.at[k], recv_sem=halo_recv.at[k],
            device_id={axis: to}, device_id_type=MESH)

    halos = ((mine > 0, mine < m - 1, halo_copy(2, edge, from_right, "col", mine - 1), from_right),
             (mine < m - 1, mine > 0, halo_copy(3, edge, from_left, "col", mine + 1), from_left),
             (me > 0, me < n - 1, halo_copy(0, vol.at[0], zhi, "depth", me - 1), zhi),
             (me < n - 1, me > 0, halo_copy(1, vol.at[depth - 1], zlo, "depth", me + 1), zlo))

    r_i = lax.broadcasted_iota(jnp.int32, (cols, cols), 0)
    c_i = lax.broadcasted_iota(jnp.int32, (cols, cols), 1)
    diff = jnp.where(r_i == c_i + 1, 1.0, 0.0) - jnp.where(r_i == c_i - 1, 1.0, 0.0)
    diff = diff.astype(jnp.bfloat16)
    zero = jnp.zeros((PAD, cols), jnp.float32)

    loads[0].wait()
    entries = table[...].astype(jnp.float32)
    sigma = entries[3:4]
    alpha = one_minus_exp(sigma)
    logs = [jnp.log(jnp.maximum(v, 1.2e-38)) * LOG2E
            for v in [entries[c:c + 1] * alpha for c in range(3)] + [sigma * LOG2E]]
    most = [jnp.max(v, axis=1, keepdims=True) for v in logs]
    least = [jnp.min(v, axis=1, keepdims=True) for v in logs]
    middle = [0.5 * (a + b) for a, b in zip(most, least)]
    grain = [jnp.maximum(a - b, 1e-3) * (1.0 / 65532.0) for a, b in zip(most, least)]
    place = [(v - o) / g for v, o, g in zip(logs, middle, grain)]

    def word(upper, lower):
        lower = jnp.floor(lower + 0.5)
        upper = jnp.floor(upper - lower * (1.0 / 65536.0) + 0.5)
        return upper.astype(jnp.int32) * 65536 + lower.astype(jnp.int32)

    words = (word(place[0], place[1]), word(place[2], place[3]))
    low = [jnp.broadcast_to(t[:, :128], (SUB, 128)) for t in words]
    high = [jnp.broadcast_to(t[:, 128:], (SUB, 128)) for t in words]
    spread = [jnp.broadcast_to(g * (1.0 / 65536.0), (SUB, cols)) for g in grain]
    sigma_middle = jnp.broadcast_to(middle[3], (SUB, cols))
    scale = [jnp.broadcast_to(jnp.exp2(o), (SUB, cols)) for o in middle[:3]]

    def widen(z, c):
        fvol[z + 1, :PAD] = zero
        fvol[z + 1, PAD + rows:] = zero
        fvol[z + 1, PAD:PAD + rows] = vol[z].astype(jnp.float32)
        return c

    for i in range(CHUNKS):
        loads[1 + i].wait()
        lax.fori_loop(i * step, (i + 1) * step, widen, 0)

    def pick(z, total):
        at = jnp.where((r_i == cols - 1) & (c_i == z), 1.0, 0.0)
        at = at + jnp.where((r_i == 0) & (c_i == depth + z), 1.0, 0.0)
        return total + jnp.dot(vol[z], at.astype(jnp.bfloat16), preferred_element_type=jnp.float32)

    edges = lax.fori_loop(0, depth, pick, jnp.zeros((rows, cols), jnp.float32), unroll=True)
    fold = cols // (2 * depth)
    short = rows // fold
    packed = edges[:short]
    for i in range(1, fold):
        packed = packed + pltpu.roll(edges[i * short:(i + 1) * short], 2 * depth * i, 1)
    edge[...] = packed.astype(jnp.bfloat16)

    def look(k, c):
        @pl.when(k == 1)
        def _():
            neighbours = (mine > 0).astype(jnp.int32) + (mine < m - 1).astype(jnp.int32)
            pl.semaphore_wait(barrier, n - 1 + neighbours)
            for sends, _, copy, _ in halos:
                pl.when(sends)(copy.start)

        load_labels(k).wait()
        u0 = pl.multiple_of(place_of(k, my_unit, units) * UNIT, UNIT)
        sums = [[jnp.zeros((SUB, cols), jnp.float32) for _ in range(4)] for _ in range(tiles)]
        def decode(z, i, first, second, gxs):
            r = slice(i * SUB, (i + 1) * SUB)
            acc0, acc1, acc2, s = sums[i]
            codes = (first, first << 16, second, second << 16)
            code0, code1, code2, code3 = [v.astype(jnp.float32) * g for v, g in zip(codes, spread)]
            w0, w1, w2 = jnp.exp2(code0 + s), jnp.exp2(code1 + s), jnp.exp2(code2 + s)
            weight[k, 0, z, r], weight[k, 1, z, r], weight[k, 2, z, r] = w0, w1, w2
            sums[i] = [acc0 + w0, acc1 + w1, acc2 + w2, s - jnp.exp2(code3 + sigma_middle)]
            at = pl.multiple_of(PAD + u0 + i * SUB, SUB)
            gy = fvol[z + 1, pl.ds(at + 1, SUB)] - fvol[z + 1, pl.ds(at - 1, SUB)]
            facing = gy * LIGHT[1]
            norm = gy * gy + 4.0
            if 0 < z < depth - 1:
                gz = fvol[z + 2, pl.ds(at, SUB)] - fvol[z, pl.ds(at, SUB)]
                facing = facing + gz * LIGHT[2]
                norm = norm + gz * gz
            across[k, z, r] = gxs[r]
            slope[k, z, r] = facing
            square[k, z, r] = norm

        places = [(z, i) for z in range(depth) for i in range(tiles)]
        gx = [jnp.dot(vol[z, pl.ds(u0, UNIT)], diff, preferred_element_type=jnp.float32) for z in range(depth)]
        got, busy, open_at = {}, [3, 0], [None, None]
        fresh = iter(places)
        decoded = 0
        while decoded < len(places):
            side = 1 if busy[1] <= busy[0] else 0
            if open_at[side] is None:
                place = next(fresh, None)
                if place is None:
                    side = 1 - side
                    if open_at[side] is None:
                        break
                else:
                    z, i = place
                    label = idx[z, pl.ds(u0 + i * SUB, SUB)]
                    open_at[side] = (place, label & 127, label < 128, [])
                    busy[side] += 1 - side
            place, lane, lower, words = open_at[side]
            words.append(take((low[1], high[1], low[0], high[0])[len(words)], lane))
            busy[side] += 1
            if len(words) == 4:
                got[place] = jnp.where(lower, words[2], words[3]), jnp.where(lower, words[0], words[1])
                open_at[side] = None
            while decoded < len(places) and places[decoded] in got:
                z, i = places[decoded]
                decode(z, i, *got[z, i], gx[z])
                decoded += 1
        for i in range(tiles):
            r = slice(i * SUB, (i + 1) * SUB)
            for c3 in range(3):
                base[k, c3, r] = sums[i][c3] * 0.25
            depths[k, r] = sums[i][3]
        return c

    lax.fori_loop(0, units, look, 0)

    for sends, receives, copy, landed in halos:
        pl.when(sends)(copy.wait_send)
        pl.when(receives)(copy.wait_recv)

        @pl.when(jnp.logical_not(receives))
        def _():
            landed[...] = jnp.zeros_like(landed)

    fvol[0, PAD:PAD + rows] = zlo[...].astype(jnp.float32)
    fvol[depth + 1, PAD:PAD + rows] = zhi[...].astype(jnp.float32)
    lane = lax.broadcasted_iota(jnp.int32, (short, cols), 1)
    packed = jnp.where(lax.rem(lane, 2 * depth) < depth, -from_left[...].astype(jnp.float32),
                       from_right[...].astype(jnp.float32))
    for i in range(fold):
        mine_here = pltpu.roll(packed, cols - 2 * depth * i, 1) if i else packed
        halo[i * short:(i + 1) * short] = jnp.where(lane < 2 * depth, mine_here, 0.0)
    lane = lax.broadcasted_iota(jnp.int32, (SUB, cols), 1)

    odd = lax.rem(me, 2)
    partner = me + 1 - 2 * odd
    behind = odd.astype(jnp.float32)
    pairs = n // 2
    my_pair = lax.div(me, 2)

    def block_of(k, j):
        return place_of(k, my_unit, units) * group + j

    def hand_over(k, j):
        slot = lax.div(block_of(k, j), 2)
        return pltpu.make_async_remote_copy(
            src_ref=part.at[k, j], dst_ref=other.at[slot], send_sem=pair_send.at[slot], recv_sem=pair_recv.at[slot],
            device_id={"depth": partner}, device_id_type=MESH)

    def deliver(to):
        slot = lax.div(to, 2)
        return pltpu.make_async_remote_copy(
            src_ref=mix.at[slot], dst_ref=recv.at[my_pair], send_sem=send_sem.at[slot], recv_sem=recv_sem.at[my_pair],
            device_id={"depth": to}, device_id_type=MESH)

    def merge(k, j, own):
        to = block_of(k, j)
        slot = lax.div(to, 2)
        hand_over(k, j).wait_recv()
        theirs = other[slot].astype(jnp.float32)
        theirs = [theirs[c * rb:(c + 1) * rb] for c in range(4)]
        front = jnp.exp2(theirs[3] * behind)
        back = jnp.exp2(own[3] * (1.0 - behind))
        both = [own[c] * front + theirs[c] * back for c in range(3)] + [own[3] + theirs[3]]
        both = jnp.concatenate(both, 0).astype(jnp.bfloat16)

        @pl.when(to != me)
        def _():
            mix[slot] = both
            deliver(to).start()

        @pl.when(to == me)
        def _():
            recv[my_pair] = both

    def shade(k):
        u0 = pl.multiple_of(place_of(k, my_unit, units) * UNIT, UNIT)
        sums = [[base[k, c3, i * SUB:(i + 1) * SUB] for c3 in range(3)] for i in range(tiles)]
        ends = [halo[pl.ds(u0 + i * SUB, SUB)] for i in range(tiles)]
        for z in range(depth):
            outer = jnp.where(lane == 0, z, jnp.where(lane == cols - 1, depth + z, cols - 1))
            for i in range(tiles):
                r = slice(i * SUB, (i + 1) * SUB)
                gx = across[k, z, r] + take(ends[i], outer)
                facing = slope[k, z, r] + gx * LIGHT[0]
                norm = square[k, z, r] + gx * gx
                if z == 0 or z == depth - 1:
                    at = pl.multiple_of(PAD + u0 + i * SUB, SUB)
                    gz = fvol[z + 2, pl.ds(at, SUB)] - fvol[z, pl.ds(at, SUB)]
                    facing = facing + gz * LIGHT[2]
                    norm = norm + gz * gz
                lit = jnp.abs(facing) * lax.rsqrt(norm)
                sums[i] = [a + weight[k, c3, z, r] * lit for c3, a in enumerate(sums[i])]
        color = [jnp.concatenate([sums[i][c3] * scale[c3] for i in range(tiles)], 0) for c3 in range(3)]
        return color + [depths[k]]

    def give(k, c):
        color = shade(k)
        for j in range(group):
            part[k, j] = jnp.concatenate([v[j * rb:(j + 1) * rb] for v in color], 0).astype(jnp.bfloat16)
            if paired:
                hand_over(k, j).start()
            else:
                pl.when(lax.rem(block_of(k, j) + me, 2) == 1)(hand_over(k, j).start)
        return c

    def keep(k, c):
        merge(k, 0, shade(k))
        return c

    def gather_pair(k, c):
        for j in range(group):
            @pl.when(lax.rem(block_of(k, j) + me, 2) == 0)
            def _():
                own = part[k, j].astype(jnp.float32)
                merge(k, j, [own[c3 * rb:(c3 + 1) * rb] for c3 in range(4)])
        return c

    paired = group == 1 and units & (units - 1) == 0
    if paired:
        lax.fori_loop(0, units // 2, give, 0)
        lax.fori_loop(units // 2, units, keep, 0)
    else:
        lax.fori_loop(0, units, give, 0)
        lax.fori_loop(0, units, gather_pair, 0)

    def arrive(k, c):
        @pl.when(k != my_pair)
        def _():
            pltpu.make_async_remote_copy(
                src_ref=mix.at[0], dst_ref=recv.at[k], send_sem=send_sem.at[0], recv_sem=recv_sem.at[k],
                device_id={"depth": 2 * k + odd}, device_id_type=MESH).wait_recv()
        return c

    lax.fori_loop(0, pairs, arrive, 0)

    def over(j, carry):
        color, s = carry
        piece = recv[j].astype(jnp.float32)
        t = jnp.exp2(s)
        color = tuple(color[c] + t * piece[c * rb:(c + 1) * rb] for c in range(3))
        return color, s + piece[3 * rb:]

    init = jnp.zeros((rb, cols), jnp.float32)
    color, s = lax.fori_loop(0, pairs, over, ((init,) * 3, init), unroll=4)
    for c in range(3):
        out[c] = color[c]
    out[3] = one_minus_exp(s * -LN2)

    def left(slot, c):
        pltpu.make_async_remote_copy(
            src_ref=part.at[0, 0], dst_ref=other.at[slot], send_sem=pair_send.at[slot], recv_sem=pair_recv.at[slot],
            device_id={"depth": partner}, device_id_type=MESH).wait_send()

        @pl.when(slot != my_pair)
        def _():
            deliver(2 * slot + odd).wait_send()
        return c

    lax.fori_loop(0, pairs, left, 0)


def on_device(volume, tf_index, tf_table):
    depth, rows, cols = volume.shape
    n = lax.axis_size("depth")
    m = lax.axis_size("col")
    vm = pl.BlockSpec(memory_space=pltpu.VMEM)
    rb = rows // n
    units, group = rows // UNIT, UNIT // rb
    return pl.pallas_call(
        functools.partial(kernel, n, m),
        out_shape=jax.ShapeDtypeStruct((4, rb, cols), jnp.float32),
        in_specs=[pl.BlockSpec(memory_space=pltpu.HBM)] * 3,
        out_specs=vm,
        scratch_shapes=[
            pltpu.VMEM(volume.shape, volume.dtype),
            pltpu.VMEM(tf_index.shape, tf_index.dtype),
            pltpu.VMEM(tf_table.shape, tf_table.dtype),
            pltpu.SemaphoreType.DMA((units + 1 + CHUNKS,)),
            pltpu.VMEM((depth + 2, rows + 2 * PAD, cols), jnp.float32),
            pltpu.VMEM((units, 3, depth, UNIT, cols), jnp.float32),
            *[pltpu.VMEM((units, depth, UNIT, cols), jnp.float32)] * 3,
            pltpu.VMEM((units, 3, UNIT, cols), jnp.float32),
            pltpu.VMEM((units, UNIT, cols), jnp.float32),
            pltpu.VMEM((units, group, 4 * rb, cols), jnp.bfloat16),
            *[pltpu.VMEM((n // 2, 4 * rb, cols), jnp.bfloat16)] * 3,
            *[pltpu.VMEM((2 * rows * depth // cols, cols), jnp.bfloat16)] * 3,
            *[pltpu.VMEM((rows, cols), jnp.bfloat16)] * 2,
            pltpu.VMEM((rows, cols), jnp.float32),
            *[pltpu.SemaphoreType.DMA((n // 2,))] * 4,
            pltpu.SemaphoreType.DMA((4,)),
            pltpu.SemaphoreType.DMA((4,)),
        ],
        compiler_params=pltpu.CompilerParams(
            collective_id=0, has_side_effects=True, vmem_limit_bytes=53 * 1024 * 1024),
    )(volume, tf_index, tf_table)


def solution(mesh):
    in_specs = (P("depth", None, "col"), P("depth", None, "col"), P())
    out_specs = P(None, "depth", "col")
    return jax.shard_map(
        on_device, mesh=mesh, in_specs=in_specs, out_specs=out_specs, check_vma=False
    )
```

```python
import functools

import jax
import jax.numpy as jnp
from jax import lax
from jax.experimental import pallas as pl
from jax.experimental.pallas import tpu as pltpu
from jax.sharding import PartitionSpec as P

LIGHT = (0.75 * 0.36, 0.75 * 0.48, 0.75 * 0.8)
LOG2E = 1.4426950408889634
LN2 = 0.6931471805599453
PAD = 8
SUB = 8
UNIT = 32
CHUNKS = 4
MESH = pl.DeviceIdType.MESH


def one_minus_exp(x):
    series = x * (1.0 - x * (0.5 - x * (1.0 / 6.0 - x * (1.0 / 24.0 - x * (1.0 / 120.0)))))
    return jnp.where(x < 0.125, series, 1.0 - jnp.exp(-x))


def place_of(k, mine, count):
    if count & (count - 1):
        return lax.rem(mine + 1 + k, count)
    half = count // 2
    mask, out = jnp.where(k < half, count - 1 - 2 * k, 2 * (count - 1 - k)), 0
    for i in range(count.bit_length() - 1):
        out = out + lax.rem(lax.div(mine, 1 << i) + lax.div(mask, 1 << i), 2) * (1 << i)
    return out


def take(row, lane):
    return jnp.take_along_axis(row, lane, axis=1, mode="promise_in_bounds")


def kernel(n, m, vol_hbm, idx_hbm, table_hbm, out, vol, idx, table, load_sem, fvol, weight, across, slope, square, base, depths,
           part, other, mix, recv, edge, from_left, from_right, zlo, zhi, halo, pair_send, pair_recv, send_sem, recv_sem, halo_send, halo_recv):
    depth, rows, cols = vol.shape
    rb = rows // n
    group = UNIT // rb
    units = rows // UNIT
    tiles = UNIT // SUB
    me = lax.axis_index("depth")
    mine = lax.axis_index("col")
    my_unit = lax.div(me, group)

    def load_labels(k):
        at = pl.ds(pl.multiple_of(place_of(k, my_unit, units) * UNIT, UNIT), UNIT)
        return pltpu.make_async_copy(idx_hbm.at[:, at], idx.at[:, at], load_sem.at[k])

    step = depth // CHUNKS
    loads = [pltpu.make_async_copy(table_hbm, table, load_sem.at[units])]
    for i in range(CHUNKS):
        at = pl.ds(i * step, step)
        loads.append(pltpu.make_async_copy(vol_hbm.at[at], vol.at[at], load_sem.at[units + 1 + i]))
    for load in loads:
        load.start()

    barrier = pltpu.get_barrier_semaphore()

    def greet(k, c):
        pl.semaphore_signal(barrier, inc=1, device_id={"depth": lax.rem(me + 1 + k, n)}, device_id_type=MESH)
        return c

    lax.fori_loop(0, n - 1, greet, 0, unroll=True)
    for there, side in ((mine > 0, -1), (mine < m - 1, 1)):
        @pl.when(there)
        def _():
            pl.semaphore_signal(barrier, inc=1, device_id={"col": mine + side}, device_id_type=MESH)

    lax.fori_loop(0, units, lambda k, c: (load_labels(k).start(), c)[1], 0, unroll=True)

    def halo_copy(k, src, dst, axis, to):
        return pltpu.make_async_remote_copy(
            src_ref=src, dst_ref=dst, send_sem=halo_send.at[k], recv_sem=halo_recv.at[k],
            device_id={axis: to}, device_id_type=MESH)

    halos = ((me > 0, me < n - 1, halo_copy(0, vol.at[0], zhi, "depth", me - 1), zhi),
             (me < n - 1, me > 0, halo_copy(1, vol.at[depth - 1], zlo, "depth", me + 1), zlo),
             (mine > 0, mine < m - 1, halo_copy(2, edge, from_right, "col", mine - 1), from_right),
             (mine < m - 1, mine > 0, halo_copy(3, edge, from_left, "col", mine + 1), from_left))

    r_i = lax.broadcasted_iota(jnp.int32, (cols, cols), 0)
    c_i = lax.broadcasted_iota(jnp.int32, (cols, cols), 1)
    diff = jnp.where(r_i == c_i + 1, 1.0, 0.0) - jnp.where(r_i == c_i - 1, 1.0, 0.0)
    diff = diff.astype(jnp.bfloat16)
    zero = jnp.zeros((PAD, cols), jnp.float32)

    loads[0].wait()
    entries = table[...].astype(jnp.float32)
    sigma = entries[3:4]
    alpha = one_minus_exp(sigma)
    logs = [jnp.log(jnp.maximum(v, 1.2e-38)) * LOG2E
            for v in [entries[c:c + 1] * alpha for c in range(3)] + [sigma * LOG2E]]
    most = [jnp.max(v, axis=1, keepdims=True) for v in logs]
    least = [jnp.min(v, axis=1, keepdims=True) for v in logs]
    middle = [0.5 * (a + b) for a, b in zip(most, least)]
    grain = [jnp.maximum(a - b, 1e-3) * (1.0 / 65532.0) for a, b in zip(most, least)]
    place = [(v - o) / g for v, o, g in zip(logs, middle, grain)]

    def word(upper, lower):
        lower = jnp.floor(lower + 0.5)
        upper = jnp.floor(upper - lower * (1.0 / 65536.0) + 0.5)
        return upper.astype(jnp.int32) * 65536 + lower.astype(jnp.int32)

    words = (word(place[0], place[1]), word(place[2], place[3]))
    low = [jnp.broadcast_to(t[:, :128], (SUB, 128)) for t in words]
    high = [jnp.broadcast_to(t[:, 128:], (SUB, 128)) for t in words]
    spread = [jnp.broadcast_to(g * (1.0 / 65536.0), (SUB, cols)) for g in grain]
    sigma_middle = jnp.broadcast_to(middle[3], (SUB, cols))
    scale = [jnp.broadcast_to(jnp.exp2(o), (SUB, cols)) for o in middle[:3]]

    def widen(z, c):
        fvol[z + 1, :PAD] = zero
        fvol[z + 1, PAD + rows:] = zero
        fvol[z + 1, PAD:PAD + rows] = vol[z].astype(jnp.float32)
        return c

    for i in range(CHUNKS):
        loads[1 + i].wait()
        lax.fori_loop(i * step, (i + 1) * step, widen, 0)

    def pick(z, total):
        at = jnp.where((r_i == cols - 1) & (c_i == z), 1.0, 0.0)
        at = at + jnp.where((r_i == 0) & (c_i == depth + z), 1.0, 0.0)
        return total + jnp.dot(vol[z], at.astype(jnp.bfloat16), preferred_element_type=jnp.float32)

    fold = cols // (2 * depth)
    short = rows // fold

    def pack_edges():
        edges = lax.fori_loop(0, depth, pick, jnp.zeros((rows, cols), jnp.float32), unroll=True)
        packed = edges[:short]
        for i in range(1, fold):
            packed = packed + pltpu.roll(edges[i * short:(i + 1) * short], 2 * depth * i, 1)
        edge[...] = packed.astype(jnp.bfloat16)

    def look(k, c):
        @pl.when(k == 1)
        def _():
            pack_edges()
            neighbours = (mine > 0).astype(jnp.int32) + (mine < m - 1).astype(jnp.int32)
            pl.semaphore_wait(barrier, n - 1 + neighbours)
            for sends, _, copy, _ in halos:
                pl.when(sends)(copy.start)

        load_labels(k).wait()
        u0 = pl.multiple_of(place_of(k, my_unit, units) * UNIT, UNIT)
        sums = [[jnp.zeros((SUB, cols), jnp.float32) for _ in range(4)] for _ in range(tiles)]
        def decode(z, i, first, second, gxs):
            r = slice(i * SUB, (i + 1) * SUB)
            acc0, acc1, acc2, s = sums[i]
            codes = (first, first << 16, second, second << 16)
            code0, code1, code2, code3 = [v.astype(jnp.float32) * g for v, g in zip(codes, spread)]
            w0, w1, w2 = jnp.exp2(code0 + s), jnp.exp2(code1 + s), jnp.exp2(code2 + s)
            weight[k, 0, z, r], weight[k, 1, z, r], weight[k, 2, z, r] = w0, w1, w2
            sums[i] = [acc0 + w0, acc1 + w1, acc2 + w2, s - jnp.exp2(code3 + sigma_middle)]
            at = pl.multiple_of(PAD + u0 + i * SUB, SUB)
            gy = fvol[z + 1, pl.ds(at + 1, SUB)] - fvol[z + 1, pl.ds(at - 1, SUB)]
            facing = gy * LIGHT[1]
            norm = gy * gy + 4.0
            if 0 < z < depth - 1:
                gz = fvol[z + 2, pl.ds(at, SUB)] - fvol[z, pl.ds(at, SUB)]
                facing = facing + gz * LIGHT[2]
                norm = norm + gz * gz
            across[k, z, r] = gxs[r]
            slope[k, z, r] = facing
            square[k, z, r] = norm

        places = [(z, i) for z in range(depth) for i in range(tiles)]
        gx = [jnp.dot(vol[z, pl.ds(u0, UNIT)], diff, preferred_element_type=jnp.float32) for z in range(depth)]
        got, busy, open_at = {}, [3, 0], [None, None]
        fresh = iter(places)
        decoded = 0
        while decoded < len(places):
            side = 1 if busy[1] <= busy[0] else 0
            if open_at[side] is None:
                place = next(fresh, None)
                if place is None:
                    side = 1 - side
                    if open_at[side] is None:
                        break
                else:
                    z, i = place
                    label = idx[z, pl.ds(u0 + i * SUB, SUB)]
                    open_at[side] = (place, label & 127, label < 128, [])
                    busy[side] += 1 - side
            place, lane, lower, words = open_at[side]
            words.append(take((low[1], high[1], low[0], high[0])[len(words)], lane))
            busy[side] += 1
            if len(words) == 4:
                got[place] = jnp.where(lower, words[2], words[3]), jnp.where(lower, words[0], words[1])
                open_at[side] = None
            while decoded < len(places) and places[decoded] in got:
                z, i = places[decoded]
                decode(z, i, *got[z, i], gx[z])
                decoded += 1
        for i in range(tiles):
            r = slice(i * SUB, (i + 1) * SUB)
            for c3 in range(3):
                base[k, c3, r] = sums[i][c3] * 0.25
            depths[k, r] = sums[i][3]
        return c

    lax.fori_loop(0, units, look, 0)

    for sends, receives, copy, landed in halos:
        pl.when(sends)(copy.wait_send)
        pl.when(receives)(copy.wait_recv)

        @pl.when(jnp.logical_not(receives))
        def _():
            landed[...] = jnp.zeros_like(landed)

    fvol[0, PAD:PAD + rows] = zlo[...].astype(jnp.float32)
    fvol[depth + 1, PAD:PAD + rows] = zhi[...].astype(jnp.float32)
    lane = lax.broadcasted_iota(jnp.int32, (short, cols), 1)
    packed = jnp.where(lax.rem(lane, 2 * depth) < depth, -from_left[...].astype(jnp.float32),
                       from_right[...].astype(jnp.float32))
    for i in range(fold):
        mine_here = pltpu.roll(packed, cols - 2 * depth * i, 1) if i else packed
        halo[i * short:(i + 1) * short] = jnp.where(lane < 2 * depth, mine_here, 0.0)
    lane = lax.broadcasted_iota(jnp.int32, (SUB, cols), 1)

    odd = lax.rem(me, 2)
    partner = me + 1 - 2 * odd
    behind = odd.astype(jnp.float32)
    pairs = n // 2
    my_pair = lax.div(me, 2)

    def block_of(k, j):
        return place_of(k, my_unit, units) * group + j

    def hand_over(k, j):
        slot = lax.div(block_of(k, j), 2)
        return pltpu.make_async_remote_copy(
            src_ref=part.at[k, j], dst_ref=other.at[slot], send_sem=pair_send.at[slot], recv_sem=pair_recv.at[slot],
            device_id={"depth": partner}, device_id_type=MESH)

    def deliver(to):
        slot = lax.div(to, 2)
        return pltpu.make_async_remote_copy(
            src_ref=mix.at[slot], dst_ref=recv.at[my_pair], send_sem=send_sem.at[slot], recv_sem=recv_sem.at[my_pair],
            device_id={"depth": to}, device_id_type=MESH)

    def merge(k, j, own):
        to = block_of(k, j)
        slot = lax.div(to, 2)
        hand_over(k, j).wait_recv()
        theirs = [other[slot, c * rb:(c + 1) * rb] for c in range(4)]
        front = jnp.exp2(theirs[3] * behind)
        back = jnp.exp2(own[3] * (1.0 - behind))
        both = [own[c] * front + theirs[c] * back for c in range(3)] + [own[3] + theirs[3]]
        both = jnp.concatenate(both, 0).astype(jnp.bfloat16)

        @pl.when(to != me)
        def _():
            mix[slot] = both
            deliver(to).start()

        @pl.when(to == me)
        def _():
            recv[my_pair] = both

    def shade(k):
        u0 = pl.multiple_of(place_of(k, my_unit, units) * UNIT, UNIT)
        sums = [[base[k, c3, i * SUB:(i + 1) * SUB] for c3 in range(3)] for i in range(tiles)]
        ends = [halo[pl.ds(u0 + i * SUB, SUB)] for i in range(tiles)]
        for z in range(depth):
            outer = jnp.where(lane == 0, z, jnp.where(lane == cols - 1, depth + z, cols - 1))
            for i in range(tiles):
                r = slice(i * SUB, (i + 1) * SUB)
                gx = across[k, z, r] + take(ends[i], outer)
                facing = slope[k, z, r] + gx * LIGHT[0]
                norm = square[k, z, r] + gx * gx
                if z == 0 or z == depth - 1:
                    at = pl.multiple_of(PAD + u0 + i * SUB, SUB)
                    gz = fvol[z + 2, pl.ds(at, SUB)] - fvol[z, pl.ds(at, SUB)]
                    facing = facing + gz * LIGHT[2]
                    norm = norm + gz * gz
                lit = jnp.abs(facing) * lax.rsqrt(norm)
                sums[i] = [a + weight[k, c3, z, r] * lit for c3, a in enumerate(sums[i])]
        color = [jnp.concatenate([sums[i][c3] * scale[c3] for i in range(tiles)], 0) for c3 in range(3)]
        return color + [depths[k]]

    def give(k, c):
        color = shade(k)
        for j in range(group):
            part[k, j] = jnp.concatenate([v[j * rb:(j + 1) * rb] for v in color], 0)
            if paired:
                hand_over(k, j).start()
            else:
                pl.when(lax.rem(block_of(k, j) + me, 2) == 1)(hand_over(k, j).start)
        return c

    def keep(k, c):
        merge(k, 0, shade(k))
        return c

    def gather_pair(k, c):
        for j in range(group):
            @pl.when(lax.rem(block_of(k, j) + me, 2) == 0)
            def _():
                merge(k, j, [part[k, j, c3 * rb:(c3 + 1) * rb] for c3 in range(4)])
        return c

    paired = group == 1 and units & (units - 1) == 0
    if paired:
        lax.fori_loop(0, units // 2, give, 0)
        lax.fori_loop(units // 2, units, keep, 0)
    else:
        lax.fori_loop(0, units, give, 0)
        lax.fori_loop(0, units, gather_pair, 0)

    def arrive(k, c):
        @pl.when(k != my_pair)
        def _():
            pltpu.make_async_remote_copy(
                src_ref=mix.at[0], dst_ref=recv.at[k], send_sem=send_sem.at[0], recv_sem=recv_sem.at[k],
                device_id={"depth": 2 * k + odd}, device_id_type=MESH).wait_recv()
        return c

    lax.fori_loop(0, pairs, arrive, 0)

    def over(j, carry):
        color, s = carry
        piece = recv[j].astype(jnp.float32)
        t = jnp.exp2(s)
        color = tuple(color[c] + t * piece[c * rb:(c + 1) * rb] for c in range(3))
        return color, s + piece[3 * rb:]

    init = jnp.zeros((rb, cols), jnp.float32)
    color, s = lax.fori_loop(0, pairs, over, ((init,) * 3, init), unroll=4)
    for c in range(3):
        out[c] = color[c]
    out[3] = one_minus_exp(s * -LN2)

    def left(slot, c):
        pltpu.make_async_remote_copy(
            src_ref=part.at[0, 0], dst_ref=other.at[slot], send_sem=pair_send.at[slot], recv_sem=pair_recv.at[slot],
            device_id={"depth": partner}, device_id_type=MESH).wait_send()

        @pl.when(slot != my_pair)
        def _():
            deliver(2 * slot + odd).wait_send()
        return c

    lax.fori_loop(0, pairs, left, 0)


def on_device(volume, tf_index, tf_table):
    depth, rows, cols = volume.shape
    n = lax.axis_size("depth")
    m = lax.axis_size("col")
    vm = pl.BlockSpec(memory_space=pltpu.VMEM)
    rb = rows // n
    units, group = rows // UNIT, UNIT // rb
    return pl.pallas_call(
        functools.partial(kernel, n, m),
        out_shape=jax.ShapeDtypeStruct((4, rb, cols), jnp.float32),
        in_specs=[pl.BlockSpec(memory_space=pltpu.HBM)] * 3,
        out_specs=vm,
        scratch_shapes=[
            pltpu.VMEM(volume.shape, volume.dtype),
            pltpu.VMEM(tf_index.shape, tf_index.dtype),
            pltpu.VMEM(tf_table.shape, tf_table.dtype),
            pltpu.SemaphoreType.DMA((units + 1 + CHUNKS,)),
            pltpu.VMEM((depth + 2, rows + 2 * PAD, cols), jnp.float32),
            pltpu.VMEM((units, 3, depth, UNIT, cols), jnp.float32),
            *[pltpu.VMEM((units, depth, UNIT, cols), jnp.float32)] * 3,
            pltpu.VMEM((units, 3, UNIT, cols), jnp.float32),
            pltpu.VMEM((units, UNIT, cols), jnp.float32),
            pltpu.VMEM((units, group, 4 * rb, cols), jnp.float32),
            pltpu.VMEM((n // 2, 4 * rb, cols), jnp.float32),
            *[pltpu.VMEM((n // 2, 4 * rb, cols), jnp.bfloat16)] * 2,
            *[pltpu.VMEM((2 * rows * depth // cols, cols), jnp.bfloat16)] * 3,
            *[pltpu.VMEM((rows, cols), jnp.bfloat16)] * 2,
            pltpu.VMEM((rows, cols), jnp.float32),
            *[pltpu.SemaphoreType.DMA((n // 2,))] * 4,
            pltpu.SemaphoreType.DMA((4,)),
            pltpu.SemaphoreType.DMA((4,)),
        ],
        compiler_params=pltpu.CompilerParams(
            collective_id=0, has_side_effects=True, vmem_limit_bytes=53 * 1024 * 1024),
    )(volume, tf_index, tf_table)


def solution(mesh):
    in_specs = (P("depth", None, "col"), P("depth", None, "col"), P())
    out_specs = P(None, "depth", "col")
    return jax.shard_map(
        on_device, mesh=mesh, in_specs=in_specs, out_specs=out_specs, check_vma=False
    )
```

```python
import functools

import jax
import jax.numpy as jnp
from jax import lax
from jax.experimental import pallas as pl
from jax.experimental.pallas import tpu as pltpu
from jax.sharding import PartitionSpec as P

LIGHT = (0.75 * 0.36, 0.75 * 0.48, 0.75 * 0.8)
LOG2E = 1.4426950408889634
LN2 = 0.6931471805599453
PAD = 8
SUB = 8
UNIT = 32
CHUNKS = 4
MESH = pl.DeviceIdType.MESH


def one_minus_exp(x):
    series = x * (1.0 - x * (0.5 - x * (1.0 / 6.0 - x * (1.0 / 24.0 - x * (1.0 / 120.0)))))
    return jnp.where(x < 0.125, series, 1.0 - jnp.exp(-x))


def place_of(k, mine, count):
    if count & (count - 1):
        return lax.rem(mine + 1 + k, count)
    half = count // 2
    mask, out = jnp.where(k < half, count - 1 - 2 * k, 2 * (count - 1 - k)), 0
    for i in range(count.bit_length() - 1):
        out = out + lax.rem(lax.div(mine, 1 << i) + lax.div(mask, 1 << i), 2) * (1 << i)
    return out


def take(row, lane):
    return jnp.take_along_axis(row, lane, axis=1, mode="promise_in_bounds")


def kernel(n, m, vol_hbm, idx_hbm, table_hbm, out, vol, idx, table, load_sem, fvol, weight, across, slope, square, base, depths,
           part, other, mix, recv, edge, from_left, from_right, zlo, zhi, halo, pair_send, pair_recv, send_sem, recv_sem, halo_send, halo_recv):
    depth, rows, cols = vol.shape
    rb = rows // n
    group = UNIT // rb
    units = rows // UNIT
    tiles = UNIT // SUB
    me = lax.axis_index("depth")
    mine = lax.axis_index("col")
    my_unit = lax.div(me, group)

    def start_of(k):
        return place_of(jnp.minimum(k, units - 1), my_unit, units) * UNIT

    def load_labels(k, start):
        at = pl.ds(pl.multiple_of(start, UNIT), UNIT)
        return pltpu.make_async_copy(idx_hbm.at[:, at], idx.at[:, at], load_sem.at[k])

    step = depth // CHUNKS
    loads = [pltpu.make_async_copy(table_hbm, table, load_sem.at[units])]
    for i in range(CHUNKS):
        at = pl.ds(i * step, step)
        loads.append(pltpu.make_async_copy(vol_hbm.at[at], vol.at[at], load_sem.at[units + 1 + i]))
    for load in loads:
        load.start()

    barrier = pltpu.get_barrier_semaphore()

    def greet(k, c):
        pl.semaphore_signal(barrier, inc=1, device_id={"depth": lax.rem(me + 1 + k, n)}, device_id_type=MESH)
        return c

    lax.fori_loop(0, n - 1, greet, 0, unroll=True)
    for there, side in ((mine > 0, -1), (mine < m - 1, 1)):
        @pl.when(there)
        def _():
            pl.semaphore_signal(barrier, inc=1, device_id={"col": mine + side}, device_id_type=MESH)

    lax.fori_loop(0, units, lambda k, c: (load_labels(k, start_of(k)).start(), c)[1], 0, unroll=True)

    def halo_copy(k, src, dst, axis, to):
        return pltpu.make_async_remote_copy(
            src_ref=src, dst_ref=dst, send_sem=halo_send.at[k], recv_sem=halo_recv.at[k],
            device_id={axis: to}, device_id_type=MESH)

    halos = ((me > 0, me < n - 1, halo_copy(0, vol.at[0], zhi, "depth", me - 1), zhi),
             (me < n - 1, me > 0, halo_copy(1, vol.at[depth - 1], zlo, "depth", me + 1), zlo),
             (mine > 0, mine < m - 1, halo_copy(2, edge, from_right, "col", mine - 1), from_right),
             (mine < m - 1, mine > 0, halo_copy(3, edge, from_left, "col", mine + 1), from_left))

    r_i = lax.broadcasted_iota(jnp.int32, (cols, cols), 0)
    c_i = lax.broadcasted_iota(jnp.int32, (cols, cols), 1)
    diff = jnp.where(r_i == c_i + 1, 1.0, 0.0) - jnp.where(r_i == c_i - 1, 1.0, 0.0)
    diff = diff.astype(jnp.bfloat16)
    zero = jnp.zeros((PAD, cols), jnp.float32)

    loads[0].wait()
    entries = table[...].astype(jnp.float32)
    sigma = entries[3:4]
    alpha = one_minus_exp(sigma)
    logs = [jnp.log(jnp.maximum(v, 1.2e-38)) * LOG2E
            for v in [entries[c:c + 1] * alpha for c in range(3)] + [sigma * LOG2E]]
    most = [jnp.max(v, axis=1, keepdims=True) for v in logs]
    least = [jnp.min(v, axis=1, keepdims=True) for v in logs]
    middle = [0.5 * (a + b) for a, b in zip(most, least)]
    grain = [jnp.maximum(a - b, 1e-3) * (1.0 / 65532.0) for a, b in zip(most, least)]
    place = [(v - o) / g for v, o, g in zip(logs, middle, grain)]

    def word(upper, lower):
        lower = jnp.floor(lower + 0.5)
        upper = jnp.floor(upper - lower * (1.0 / 65536.0) + 0.5)
        return upper.astype(jnp.int32) * 65536 + lower.astype(jnp.int32)

    words = (word(place[0], place[1]), word(place[2], place[3]))
    low = [jnp.broadcast_to(t[:, :128], (SUB, 128)) for t in words]
    high = [jnp.broadcast_to(t[:, 128:], (SUB, 128)) for t in words]
    spread = [jnp.broadcast_to(g * (1.0 / 65536.0), (SUB, cols)) for g in grain]
    sigma_middle = jnp.broadcast_to(middle[3], (SUB, cols))
    scale = [jnp.broadcast_to(jnp.exp2(o), (SUB, cols)) for o in middle[:3]]

    def widen(z, c):
        fvol[z + 1, :PAD] = zero
        fvol[z + 1, PAD + rows:] = zero
        fvol[z + 1, PAD:PAD + rows] = vol[z].astype(jnp.float32)
        return c

    for i in range(CHUNKS):
        loads[1 + i].wait()
        lax.fori_loop(i * step, (i + 1) * step, widen, 0)

    def pick(z, total):
        at = jnp.where((r_i == cols - 1) & (c_i == z), 1.0, 0.0)
        at = at + jnp.where((r_i == 0) & (c_i == depth + z), 1.0, 0.0)
        return total + jnp.dot(vol[z], at.astype(jnp.bfloat16), preferred_element_type=jnp.float32)

    fold = cols // (2 * depth)
    short = rows // fold

    def pack_edges():
        edges = lax.fori_loop(0, depth, pick, jnp.zeros((rows, cols), jnp.float32), unroll=True)
        packed = edges[:short]
        for i in range(1, fold):
            packed = packed + pltpu.roll(edges[i * short:(i + 1) * short], 2 * depth * i, 1)
        edge[...] = packed.astype(jnp.bfloat16)

    def look(k, start):
        @pl.when(k == 1)
        def _():
            pack_edges()
            neighbours = (mine > 0).astype(jnp.int32) + (mine < m - 1).astype(jnp.int32)
            pl.semaphore_wait(barrier, n - 1 + neighbours)
            for sends, _, copy, _ in halos:
                pl.when(sends)(copy.start)

        load_labels(k, start).wait()
        u0 = pl.multiple_of(start, UNIT)
        sums = [[jnp.zeros((SUB, cols), jnp.float32) for _ in range(4)] for _ in range(tiles)]
        def decode(z, i, first, second, gxs):
            r = slice(i * SUB, (i + 1) * SUB)
            acc0, acc1, acc2, s = sums[i]
            codes = (first, first << 16, second, second << 16)
            code0, code1, code2, code3 = [v.astype(jnp.float32) * g for v, g in zip(codes, spread)]
            w0, w1, w2 = jnp.exp2(code0 + s), jnp.exp2(code1 + s), jnp.exp2(code2 + s)
            weight[k, 0, z, r], weight[k, 1, z, r], weight[k, 2, z, r] = w0, w1, w2
            sums[i] = [acc0 + w0, acc1 + w1, acc2 + w2, s - jnp.exp2(code3 + sigma_middle)]
            at = pl.multiple_of(PAD + u0 + i * SUB, SUB)
            gy = fvol[z + 1, pl.ds(at + 1, SUB)] - fvol[z + 1, pl.ds(at - 1, SUB)]
            facing = gy * LIGHT[1]
            norm = gy * gy + 4.0
            if 0 < z < depth - 1:
                gz = fvol[z + 2, pl.ds(at, SUB)] - fvol[z, pl.ds(at, SUB)]
                facing = facing + gz * LIGHT[2]
                norm = norm + gz * gz
            across[k, z, r] = gxs[r]
            slope[k, z, r] = facing
            square[k, z, r] = norm

        places = [(z, i) for z in range(depth) for i in range(tiles)]
        gx = [jnp.dot(vol[z, pl.ds(u0, UNIT)], diff, preferred_element_type=jnp.float32) for z in range(depth)]
        got, busy, open_at = {}, [3, 0], [None, None]
        fresh = iter(places)
        decoded = 0
        while decoded < len(places):
            side = 1 if busy[1] <= busy[0] else 0
            if open_at[side] is None:
                place = next(fresh, None)
                if place is None:
                    side = 1 - side
                    if open_at[side] is None:
                        break
                else:
                    z, i = place
                    label = idx[z, pl.ds(u0 + i * SUB, SUB)]
                    open_at[side] = (place, label & 127, label < 128, [])
                    busy[side] += 1 - side
            place, lane, lower, words = open_at[side]
            words.append(take((low[1], high[1], low[0], high[0])[len(words)], lane))
            busy[side] += 1
            if len(words) == 4:
                got[place] = jnp.where(lower, words[2], words[3]), jnp.where(lower, words[0], words[1])
                open_at[side] = None
            while decoded < len(places) and places[decoded] in got:
                z, i = places[decoded]
                decode(z, i, *got[z, i], gx[z])
                decoded += 1
        for i in range(tiles):
            r = slice(i * SUB, (i + 1) * SUB)
            for c3 in range(3):
                base[k, c3, r] = sums[i][c3] * 0.25
            depths[k, r] = sums[i][3]
        return start_of(k + 1)

    lax.fori_loop(0, units, look, start_of(0))

    for sends, receives, copy, landed in halos:
        pl.when(sends)(copy.wait_send)
        pl.when(receives)(copy.wait_recv)

        @pl.when(jnp.logical_not(receives))
        def _():
            landed[...] = jnp.zeros_like(landed)

    fvol[0, PAD:PAD + rows] = zlo[...].astype(jnp.float32)
    fvol[depth + 1, PAD:PAD + rows] = zhi[...].astype(jnp.float32)
    lane = lax.broadcasted_iota(jnp.int32, (short, cols), 1)
    packed = jnp.where(lax.rem(lane, 2 * depth) < depth, -from_left[...].astype(jnp.float32),
                       from_right[...].astype(jnp.float32))
    for i in range(fold):
        mine_here = pltpu.roll(packed, cols - 2 * depth * i, 1) if i else packed
        halo[i * short:(i + 1) * short] = jnp.where(lane < 2 * depth, mine_here, 0.0)
    lane = lax.broadcasted_iota(jnp.int32, (SUB, cols), 1)

    odd = lax.rem(me, 2)
    partner = me + 1 - 2 * odd
    behind = odd.astype(jnp.float32)
    pairs = n // 2
    my_pair = lax.div(me, 2)

    def block_of(k, j):
        return place_of(k, my_unit, units) * group + j

    def hand_over(k, j):
        slot = lax.div(block_of(k, j), 2)
        return pltpu.make_async_remote_copy(
            src_ref=part.at[k, j], dst_ref=other.at[slot], send_sem=pair_send.at[slot], recv_sem=pair_recv.at[slot],
            device_id={"depth": partner}, device_id_type=MESH)

    def deliver(to):
        slot = lax.div(to, 2)
        return pltpu.make_async_remote_copy(
            src_ref=mix.at[slot], dst_ref=recv.at[my_pair], send_sem=send_sem.at[slot], recv_sem=recv_sem.at[my_pair],
            device_id={"depth": to}, device_id_type=MESH)

    def merge(k, j, own):
        to = block_of(k, j)
        slot = lax.div(to, 2)
        hand_over(k, j).wait_recv()
        theirs = [other[slot, c * rb:(c + 1) * rb] for c in range(4)]
        front = jnp.exp2(theirs[3] * behind)
        back = jnp.exp2(own[3] * (1.0 - behind))
        both = [own[c] * front + theirs[c] * back for c in range(3)] + [own[3] + theirs[3]]
        both = jnp.concatenate(both, 0).astype(jnp.bfloat16)

        @pl.when(to != me)
        def _():
            mix[slot] = both
            deliver(to).start()

        @pl.when(to == me)
        def _():
            recv[my_pair] = both

    def shade(k, start):
        u0 = pl.multiple_of(start, UNIT)
        sums = [[base[k, c3, i * SUB:(i + 1) * SUB] for c3 in range(3)] for i in range(tiles)]
        ends = [halo[pl.ds(u0 + i * SUB, SUB)] for i in range(tiles)]
        for z in range(depth):
            outer = jnp.where(lane == 0, z, jnp.where(lane == cols - 1, depth + z, cols - 1))
            for i in range(tiles):
                r = slice(i * SUB, (i + 1) * SUB)
                gx = across[k, z, r] + take(ends[i], outer)
                facing = slope[k, z, r] + gx * LIGHT[0]
                norm = square[k, z, r] + gx * gx
                if z == 0 or z == depth - 1:
                    at = pl.multiple_of(PAD + u0 + i * SUB, SUB)
                    gz = fvol[z + 2, pl.ds(at, SUB)] - fvol[z, pl.ds(at, SUB)]
                    facing = facing + gz * LIGHT[2]
                    norm = norm + gz * gz
                lit = jnp.abs(facing) * lax.rsqrt(norm)
                sums[i] = [a + weight[k, c3, z, r] * lit for c3, a in enumerate(sums[i])]
        color = [jnp.concatenate([sums[i][c3] * scale[c3] for i in range(tiles)], 0) for c3 in range(3)]
        return color + [depths[k]]

    def give(k, start):
        color = shade(k, start)
        for j in range(group):
            part[k, j] = jnp.concatenate([v[j * rb:(j + 1) * rb] for v in color], 0)
            if paired:
                hand_over(k, j).start()
            else:
                pl.when(lax.rem(block_of(k, j) + me, 2) == 1)(hand_over(k, j).start)
        return start_of(k + 1)

    def keep(k, start):
        merge(k, 0, shade(k, start))
        return start_of(k + 1)

    def gather_pair(k, c):
        for j in range(group):
            @pl.when(lax.rem(block_of(k, j) + me, 2) == 0)
            def _():
                merge(k, j, [part[k, j, c3 * rb:(c3 + 1) * rb] for c3 in range(4)])
        return c

    paired = group == 1 and units & (units - 1) == 0
    if paired:
        start = lax.fori_loop(0, units // 2, give, start_of(0))
        lax.fori_loop(units // 2, units, keep, start)
    else:
        lax.fori_loop(0, units, give, start_of(0))
        lax.fori_loop(0, units, gather_pair, 0)

    def arrive(k, c):
        @pl.when(k != my_pair)
        def _():
            pltpu.make_async_remote_copy(
                src_ref=mix.at[0], dst_ref=recv.at[k], send_sem=send_sem.at[0], recv_sem=recv_sem.at[k],
                device_id={"depth": 2 * k + odd}, device_id_type=MESH).wait_recv()
        return c

    lax.fori_loop(0, pairs, arrive, 0)

    def over(j, carry):
        color, s = carry
        piece = recv[j].astype(jnp.float32)
        t = jnp.exp2(s)
        color = tuple(color[c] + t * piece[c * rb:(c + 1) * rb] for c in range(3))
        return color, s + piece[3 * rb:]

    init = jnp.zeros((rb, cols), jnp.float32)
    color, s = lax.fori_loop(0, pairs, over, ((init,) * 3, init), unroll=4)
    for c in range(3):
        out[c] = color[c]
    out[3] = one_minus_exp(s * -LN2)

    def left(slot, c):
        pltpu.make_async_remote_copy(
            src_ref=part.at[0, 0], dst_ref=other.at[slot], send_sem=pair_send.at[slot], recv_sem=pair_recv.at[slot],
            device_id={"depth": partner}, device_id_type=MESH).wait_send()

        @pl.when(slot != my_pair)
        def _():
            deliver(2 * slot + odd).wait_send()
        return c

    lax.fori_loop(0, pairs, left, 0)


def on_device(volume, tf_index, tf_table):
    depth, rows, cols = volume.shape
    n = lax.axis_size("depth")
    m = lax.axis_size("col")
    vm = pl.BlockSpec(memory_space=pltpu.VMEM)
    rb = rows // n
    units, group = rows // UNIT, UNIT // rb
    return pl.pallas_call(
        functools.partial(kernel, n, m),
        out_shape=jax.ShapeDtypeStruct((4, rb, cols), jnp.float32),
        in_specs=[pl.BlockSpec(memory_space=pltpu.HBM)] * 3,
        out_specs=vm,
        scratch_shapes=[
            pltpu.VMEM(volume.shape, volume.dtype),
            pltpu.VMEM(tf_index.shape, tf_index.dtype),
            pltpu.VMEM(tf_table.shape, tf_table.dtype),
            pltpu.SemaphoreType.DMA((units + 1 + CHUNKS,)),
            pltpu.VMEM((depth + 2, rows + 2 * PAD, cols), jnp.float32),
            pltpu.VMEM((units, 3, depth, UNIT, cols), jnp.float32),
            *[pltpu.VMEM((units, depth, UNIT, cols), jnp.float32)] * 3,
            pltpu.VMEM((units, 3, UNIT, cols), jnp.float32),
            pltpu.VMEM((units, UNIT, cols), jnp.float32),
            pltpu.VMEM((units, group, 4 * rb, cols), jnp.float32),
            pltpu.VMEM((n // 2, 4 * rb, cols), jnp.float32),
            *[pltpu.VMEM((n // 2, 4 * rb, cols), jnp.bfloat16)] * 2,
            *[pltpu.VMEM((2 * rows * depth // cols, cols), jnp.bfloat16)] * 3,
            *[pltpu.VMEM((rows, cols), jnp.bfloat16)] * 2,
            pltpu.VMEM((rows, cols), jnp.float32),
            *[pltpu.SemaphoreType.DMA((n // 2,))] * 4,
            pltpu.SemaphoreType.DMA((4,)),
            pltpu.SemaphoreType.DMA((4,)),
        ],
        compiler_params=pltpu.CompilerParams(
            collective_id=0, has_side_effects=True, vmem_limit_bytes=53 * 1024 * 1024),
    )(volume, tf_index, tf_table)


def solution(mesh):
    in_specs = (P("depth", None, "col"), P("depth", None, "col"), P())
    out_specs = P(None, "depth", "col")
    return jax.shard_map(
        on_device, mesh=mesh, in_specs=in_specs, out_specs=out_specs, check_vma=False
    )
```

```python
import functools

import jax
import jax.numpy as jnp
from jax import lax
from jax.experimental import pallas as pl
from jax.experimental.pallas import tpu as pltpu
from jax.sharding import PartitionSpec as P

LIGHT = (0.75 * 0.36, 0.75 * 0.48, 0.75 * 0.8)
LOG2E = 1.4426950408889634
LN2 = 0.6931471805599453
PAD = 8
SUB = 8
UNIT = 32
CHUNKS = 4
MESH = pl.DeviceIdType.MESH


def one_minus_exp(x):
    series = x * (1.0 - x * (0.5 - x * (1.0 / 6.0 - x * (1.0 / 24.0 - x * (1.0 / 120.0)))))
    return jnp.where(x < 0.125, series, 1.0 - jnp.exp(-x))


def place_of(k, mine, count):
    if count & (count - 1):
        return lax.rem(mine + 1 + k, count)
    half = count // 2
    mask, out = jnp.where(k < half, count - 1 - 2 * k, 2 * (count - 1 - k)), 0
    for i in range(count.bit_length() - 1):
        out = out + lax.rem(lax.div(mine, 1 << i) + lax.div(mask, 1 << i), 2) * (1 << i)
    return out


def take(row, lane):
    return jnp.take_along_axis(row, lane, axis=1, mode="promise_in_bounds")


def kernel(n, m, vol_hbm, idx_hbm, table_hbm, out, vol, idx, table, load_sem, fvol, weight, across, slope, square, base, depths,
           part, other, mix, recv, edge, from_left, from_right, zlo, zhi, halo, pair_send, pair_recv, send_sem, recv_sem, halo_send, halo_recv, vouched):
    depth, rows, cols = vol.shape
    rb = rows // n
    group = UNIT // rb
    units = rows // UNIT
    tiles = UNIT // SUB
    me = lax.axis_index("depth")
    mine = lax.axis_index("col")
    my_unit = lax.div(me, group)

    def start_of(k):
        return place_of(jnp.minimum(k, units - 1), my_unit, units) * UNIT

    def load_labels(k, start):
        at = pl.ds(pl.multiple_of(start, UNIT), UNIT)
        return pltpu.make_async_copy(idx_hbm.at[:, at], idx.at[:, at], load_sem.at[k])

    step = depth // CHUNKS
    loads = [pltpu.make_async_copy(table_hbm, table, load_sem.at[units])]
    for i in range(CHUNKS):
        at = pl.ds(i * step, step)
        loads.append(pltpu.make_async_copy(vol_hbm.at[at], vol.at[at], load_sem.at[units + 1 + i]))
    for load in loads:
        load.start()

    barrier = pltpu.get_barrier_semaphore()

    odd = lax.rem(me, 2)
    cube = n == 8

    def across_bit(i):
        return me + (1 - 2 * lax.rem(lax.div(me, 1 << i), 2)) * (1 << i)

    def greet(to):
        pl.semaphore_signal(barrier, inc=1, device_id={"depth": to}, device_id_type=MESH)

    beside = me - 1 + 2 * odd
    has_beside = jnp.where(odd == 1, me < n - 1, me > 0)
    if cube:
        for i in range(3):
            greet(across_bit(i))
        pl.when(has_beside)(lambda: greet(beside))
        greeted = 3 + has_beside.astype(jnp.int32)
    else:
        lax.fori_loop(0, n - 1, lambda k, c: (greet(lax.rem(me + 1 + k, n)), c)[1], 0)
        greeted = n - 1
    for there, side in ((mine > 0, -1), (mine < m - 1, 1)):
        @pl.when(there)
        def _():
            pl.semaphore_signal(barrier, inc=1, device_id={"col": mine + side}, device_id_type=MESH)

    lax.fori_loop(0, units, lambda k, c: (load_labels(k, start_of(k)).start(), c)[1], 0, unroll=True)

    def halo_copy(k, src, dst, axis, to):
        return pltpu.make_async_remote_copy(
            src_ref=src, dst_ref=dst, send_sem=halo_send.at[k], recv_sem=halo_recv.at[k],
            device_id={axis: to}, device_id_type=MESH)

    halos = ((me > 0, me < n - 1, halo_copy(0, vol.at[0], zhi, "depth", me - 1), zhi),
             (me < n - 1, me > 0, halo_copy(1, vol.at[depth - 1], zlo, "depth", me + 1), zlo),
             (mine > 0, mine < m - 1, halo_copy(2, edge, from_right, "col", mine - 1), from_right),
             (mine < m - 1, mine > 0, halo_copy(3, edge, from_left, "col", mine + 1), from_left))

    r_i = lax.broadcasted_iota(jnp.int32, (cols, cols), 0)
    c_i = lax.broadcasted_iota(jnp.int32, (cols, cols), 1)
    diff = jnp.where(r_i == c_i + 1, 1.0, 0.0) - jnp.where(r_i == c_i - 1, 1.0, 0.0)
    diff = diff.astype(jnp.bfloat16)
    zero = jnp.zeros((PAD, cols), jnp.float32)

    loads[0].wait()
    entries = table[...].astype(jnp.float32)
    sigma = entries[3:4]
    alpha = one_minus_exp(sigma)
    logs = [jnp.log(jnp.maximum(v, 1.2e-38)) * LOG2E
            for v in [entries[c:c + 1] * alpha for c in range(3)] + [sigma * LOG2E]]
    most = [jnp.max(v, axis=1, keepdims=True) for v in logs]
    least = [jnp.min(v, axis=1, keepdims=True) for v in logs]
    middle = [0.5 * (a + b) for a, b in zip(most, least)]
    grain = [jnp.maximum(a - b, 1e-3) * (1.0 / 65532.0) for a, b in zip(most, least)]
    place = [(v - o) / g for v, o, g in zip(logs, middle, grain)]

    def word(upper, lower):
        lower = jnp.floor(lower + 0.5)
        upper = jnp.floor(upper - lower * (1.0 / 65536.0) + 0.5)
        return upper.astype(jnp.int32) * 65536 + lower.astype(jnp.int32)

    words = (word(place[0], place[1]), word(place[2], place[3]))
    low = [jnp.broadcast_to(t[:, :128], (SUB, 128)) for t in words]
    high = [jnp.broadcast_to(t[:, 128:], (SUB, 128)) for t in words]
    spread = [jnp.broadcast_to(g * (1.0 / 65536.0), (SUB, cols)) for g in grain]
    sigma_middle = jnp.broadcast_to(middle[3], (SUB, cols))
    scale = [jnp.broadcast_to(jnp.exp2(o), (SUB, cols)) for o in middle[:3]]

    def widen(z, c):
        fvol[z + 1, :PAD] = zero
        fvol[z + 1, PAD + rows:] = zero
        fvol[z + 1, PAD:PAD + rows] = vol[z].astype(jnp.float32)
        return c

    for i in range(CHUNKS):
        loads[1 + i].wait()
        lax.fori_loop(i * step, (i + 1) * step, widen, 0)

    def pick(z, total):
        at = jnp.where((r_i == cols - 1) & (c_i == z), 1.0, 0.0)
        at = at + jnp.where((r_i == 0) & (c_i == depth + z), 1.0, 0.0)
        return total + jnp.dot(vol[z], at.astype(jnp.bfloat16), preferred_element_type=jnp.float32)

    fold = cols // (2 * depth)
    short = rows // fold

    def pack_edges():
        edges = lax.fori_loop(0, depth, pick, jnp.zeros((rows, cols), jnp.float32), unroll=True)
        packed = edges[:short]
        for i in range(1, fold):
            packed = packed + pltpu.roll(edges[i * short:(i + 1) * short], 2 * depth * i, 1)
        edge[...] = packed.astype(jnp.bfloat16)

    def look(k, start):
        @pl.when(k == 1)
        def _():
            pack_edges()
            neighbours = (mine > 0).astype(jnp.int32) + (mine < m - 1).astype(jnp.int32)
            pl.semaphore_wait(barrier, greeted + neighbours)
            if cube:
                pl.semaphore_signal(vouched, inc=1, device_id={"depth": across_bit(1)}, device_id_type=MESH)
            for sends, _, copy, _ in halos:
                pl.when(sends)(copy.start)

        load_labels(k, start).wait()
        u0 = pl.multiple_of(start, UNIT)
        sums = [[jnp.zeros((SUB, cols), jnp.float32) for _ in range(4)] for _ in range(tiles)]
        def decode(z, i, first, second, gxs):
            r = slice(i * SUB, (i + 1) * SUB)
            acc0, acc1, acc2, s = sums[i]
            codes = (first, first << 16, second, second << 16)
            code0, code1, code2, code3 = [v.astype(jnp.float32) * g for v, g in zip(codes, spread)]
            w0, w1, w2 = jnp.exp2(code0 + s), jnp.exp2(code1 + s), jnp.exp2(code2 + s)
            weight[k, 0, z, r], weight[k, 1, z, r], weight[k, 2, z, r] = w0, w1, w2
            sums[i] = [acc0 + w0, acc1 + w1, acc2 + w2, s - jnp.exp2(code3 + sigma_middle)]
            at = pl.multiple_of(PAD + u0 + i * SUB, SUB)
            gy = fvol[z + 1, pl.ds(at + 1, SUB)] - fvol[z + 1, pl.ds(at - 1, SUB)]
            facing = gy * LIGHT[1]
            norm = gy * gy + 4.0
            if 0 < z < depth - 1:
                gz = fvol[z + 2, pl.ds(at, SUB)] - fvol[z, pl.ds(at, SUB)]
                facing = facing + gz * LIGHT[2]
                norm = norm + gz * gz
            across[k, z, r] = gxs[r]
            slope[k, z, r] = facing
            square[k, z, r] = norm

        places = [(z, i) for z in range(depth) for i in range(tiles)]
        gx = [jnp.dot(vol[z, pl.ds(u0, UNIT)], diff, preferred_element_type=jnp.float32) for z in range(depth)]
        got, busy, open_at = {}, [3, 0], [None, None]
        fresh = iter(places)
        decoded = 0
        while decoded < len(places):
            side = 1 if busy[1] <= busy[0] else 0
            if open_at[side] is None:
                place = next(fresh, None)
                if place is None:
                    side = 1 - side
                    if open_at[side] is None:
                        break
                else:
                    z, i = place
                    label = idx[z, pl.ds(u0 + i * SUB, SUB)]
                    open_at[side] = (place, label & 127, label < 128, [])
                    busy[side] += 1 - side
            place, lane, lower, words = open_at[side]
            words.append(take((low[1], high[1], low[0], high[0])[len(words)], lane))
            busy[side] += 1
            if len(words) == 4:
                got[place] = jnp.where(lower, words[2], words[3]), jnp.where(lower, words[0], words[1])
                open_at[side] = None
            while decoded < len(places) and places[decoded] in got:
                z, i = places[decoded]
                decode(z, i, *got[z, i], gx[z])
                decoded += 1
        for i in range(tiles):
            r = slice(i * SUB, (i + 1) * SUB)
            for c3 in range(3):
                base[k, c3, r] = sums[i][c3] * 0.25
            depths[k, r] = sums[i][3]
        return start_of(k + 1)

    lax.fori_loop(0, units, look, start_of(0))

    for sends, receives, copy, landed in halos:
        pl.when(sends)(copy.wait_send)
        pl.when(receives)(copy.wait_recv)

        @pl.when(jnp.logical_not(receives))
        def _():
            landed[...] = jnp.zeros_like(landed)

    fvol[0, PAD:PAD + rows] = zlo[...].astype(jnp.float32)
    fvol[depth + 1, PAD:PAD + rows] = zhi[...].astype(jnp.float32)
    lane = lax.broadcasted_iota(jnp.int32, (short, cols), 1)
    packed = jnp.where(lax.rem(lane, 2 * depth) < depth, -from_left[...].astype(jnp.float32),
                       from_right[...].astype(jnp.float32))
    for i in range(fold):
        mine_here = pltpu.roll(packed, cols - 2 * depth * i, 1) if i else packed
        halo[i * short:(i + 1) * short] = jnp.where(lane < 2 * depth, mine_here, 0.0)
    lane = lax.broadcasted_iota(jnp.int32, (SUB, cols), 1)

    partner = me + 1 - 2 * odd
    behind = odd.astype(jnp.float32)
    pairs = n // 2
    my_pair = lax.div(me, 2)

    def block_of(k, j):
        return place_of(k, my_unit, units) * group + j

    def hand_over(k, j):
        slot = lax.div(block_of(k, j), 2)
        return pltpu.make_async_remote_copy(
            src_ref=part.at[k, j], dst_ref=other.at[slot], send_sem=pair_send.at[slot], recv_sem=pair_recv.at[slot],
            device_id={"depth": partner}, device_id_type=MESH)

    def deliver(to):
        slot = lax.div(to, 2)
        return pltpu.make_async_remote_copy(
            src_ref=mix.at[slot], dst_ref=recv.at[my_pair], send_sem=send_sem.at[slot], recv_sem=recv_sem.at[my_pair],
            device_id={"depth": to}, device_id_type=MESH)

    def merge(k, j, own):
        to = block_of(k, j)
        slot = lax.div(to, 2)
        hand_over(k, j).wait_recv()
        theirs = [other[slot, c * rb:(c + 1) * rb] for c in range(4)]
        front = jnp.exp2(theirs[3] * behind)
        back = jnp.exp2(own[3] * (1.0 - behind))
        both = [own[c] * front + theirs[c] * back for c in range(3)] + [own[3] + theirs[3]]
        both = jnp.concatenate(both, 0).astype(jnp.bfloat16)

        @pl.when(to != me)
        def _():
            mix[slot] = both
            deliver(to).start()

        @pl.when(to == me)
        def _():
            recv[my_pair] = both

    def shade(k, start):
        u0 = pl.multiple_of(start, UNIT)
        sums = [[base[k, c3, i * SUB:(i + 1) * SUB] for c3 in range(3)] for i in range(tiles)]
        ends = [halo[pl.ds(u0 + i * SUB, SUB)] for i in range(tiles)]
        for z in range(depth):
            outer = jnp.where(lane == 0, z, jnp.where(lane == cols - 1, depth + z, cols - 1))
            for i in range(tiles):
                r = slice(i * SUB, (i + 1) * SUB)
                gx = across[k, z, r] + take(ends[i], outer)
                facing = slope[k, z, r] + gx * LIGHT[0]
                norm = square[k, z, r] + gx * gx
                if z == 0 or z == depth - 1:
                    at = pl.multiple_of(PAD + u0 + i * SUB, SUB)
                    gz = fvol[z + 2, pl.ds(at, SUB)] - fvol[z, pl.ds(at, SUB)]
                    facing = facing + gz * LIGHT[2]
                    norm = norm + gz * gz
                lit = jnp.abs(facing) * lax.rsqrt(norm)
                sums[i] = [a + weight[k, c3, z, r] * lit for c3, a in enumerate(sums[i])]
        color = [jnp.concatenate([sums[i][c3] * scale[c3] for i in range(tiles)], 0) for c3 in range(3)]
        return color + [depths[k]]

    def give(k, start):
        color = shade(k, start)
        for j in range(group):
            part[k, j] = jnp.concatenate([v[j * rb:(j + 1) * rb] for v in color], 0)
            if paired:
                hand_over(k, j).start()
            else:
                pl.when(lax.rem(block_of(k, j) + me, 2) == 1)(hand_over(k, j).start)
        return start_of(k + 1)

    def keep(k, start):
        merge(k, 0, shade(k, start))
        return start_of(k + 1)

    def gather_pair(k, c):
        for j in range(group):
            @pl.when(lax.rem(block_of(k, j) + me, 2) == 0)
            def _():
                merge(k, j, [part[k, j, c3 * rb:(c3 + 1) * rb] for c3 in range(4)])
        return c

    paired = group == 1 and units & (units - 1) == 0
    if paired:
        start = lax.fori_loop(0, units // 2, give, start_of(0))
        if cube:
            pl.semaphore_wait(vouched, 1)
        lax.fori_loop(units // 2, units, keep, start)
    else:
        lax.fori_loop(0, units, give, start_of(0))
        if cube:
            pl.semaphore_wait(vouched, 1)
        lax.fori_loop(0, units, gather_pair, 0)

    def arrive(k, c):
        @pl.when(k != my_pair)
        def _():
            pltpu.make_async_remote_copy(
                src_ref=mix.at[0], dst_ref=recv.at[k], send_sem=send_sem.at[0], recv_sem=recv_sem.at[k],
                device_id={"depth": 2 * k + odd}, device_id_type=MESH).wait_recv()
        return c

    lax.fori_loop(0, pairs, arrive, 0)

    def over(j, carry):
        color, s = carry
        piece = recv[j].astype(jnp.float32)
        t = jnp.exp2(s)
        color = tuple(color[c] + t * piece[c * rb:(c + 1) * rb] for c in range(3))
        return color, s + piece[3 * rb:]

    init = jnp.zeros((rb, cols), jnp.float32)
    color, s = lax.fori_loop(0, pairs, over, ((init,) * 3, init), unroll=4)
    for c in range(3):
        out[c] = color[c]
    out[3] = one_minus_exp(s * -LN2)

    def left(slot, c):
        pltpu.make_async_remote_copy(
            src_ref=part.at[0, 0], dst_ref=other.at[slot], send_sem=pair_send.at[slot], recv_sem=pair_recv.at[slot],
            device_id={"depth": partner}, device_id_type=MESH).wait_send()

        @pl.when(slot != my_pair)
        def _():
            deliver(2 * slot + odd).wait_send()
        return c

    lax.fori_loop(0, pairs, left, 0)


def on_device(volume, tf_index, tf_table):
    depth, rows, cols = volume.shape
    n = lax.axis_size("depth")
    m = lax.axis_size("col")
    vm = pl.BlockSpec(memory_space=pltpu.VMEM)
    rb = rows // n
    units, group = rows // UNIT, UNIT // rb
    return pl.pallas_call(
        functools.partial(kernel, n, m),
        out_shape=jax.ShapeDtypeStruct((4, rb, cols), jnp.float32),
        in_specs=[pl.BlockSpec(memory_space=pltpu.HBM)] * 3,
        out_specs=vm,
        scratch_shapes=[
            pltpu.VMEM(volume.shape, volume.dtype),
            pltpu.VMEM(tf_index.shape, tf_index.dtype),
            pltpu.VMEM(tf_table.shape, tf_table.dtype),
            pltpu.SemaphoreType.DMA((units + 1 + CHUNKS,)),
            pltpu.VMEM((depth + 2, rows + 2 * PAD, cols), jnp.float32),
            pltpu.VMEM((units, 3, depth, UNIT, cols), jnp.float32),
            *[pltpu.VMEM((units, depth, UNIT, cols), jnp.float32)] * 3,
            pltpu.VMEM((units, 3, UNIT, cols), jnp.float32),
            pltpu.VMEM((units, UNIT, cols), jnp.float32),
            pltpu.VMEM((units, group, 4 * rb, cols), jnp.float32),
            pltpu.VMEM((n // 2, 4 * rb, cols), jnp.float32),
            *[pltpu.VMEM((n // 2, 4 * rb, cols), jnp.bfloat16)] * 2,
            *[pltpu.VMEM((2 * rows * depth // cols, cols), jnp.bfloat16)] * 3,
            *[pltpu.VMEM((rows, cols), jnp.bfloat16)] * 2,
            pltpu.VMEM((rows, cols), jnp.float32),
            *[pltpu.SemaphoreType.DMA((n // 2,))] * 4,
            pltpu.SemaphoreType.DMA((4,)),
            pltpu.SemaphoreType.DMA((4,)),
            pltpu.SemaphoreType.REGULAR,
        ],
        compiler_params=pltpu.CompilerParams(
            collective_id=0, has_side_effects=True, vmem_limit_bytes=53 * 1024 * 1024),
    )(volume, tf_index, tf_table)


def solution(mesh):
    in_specs = (P("depth", None, "col"), P("depth", None, "col"), P())
    out_specs = P(None, "depth", "col")
    return jax.shard_map(
        on_device, mesh=mesh, in_specs=in_specs, out_specs=out_specs, check_vma=False
    )
```

```python
import functools

import jax
import jax.numpy as jnp
from jax import lax
from jax.experimental import pallas as pl
from jax.experimental.pallas import tpu as pltpu
from jax.sharding import PartitionSpec as P

LIGHT = (0.75 * 0.36, 0.75 * 0.48, 0.75 * 0.8)
LOG2E = 1.4426950408889634
LN2 = 0.6931471805599453
PAD = 8
SUB = 8
UNIT = 32
CHUNKS = 2
MESH = pl.DeviceIdType.MESH


def one_minus_exp(x):
    series = x * (1.0 - x * (0.5 - x * (1.0 / 6.0 - x * (1.0 / 24.0 - x * (1.0 / 120.0)))))
    return jnp.where(x < 0.125, series, 1.0 - jnp.exp(-x))


def place_of(k, mine, count):
    if count & (count - 1):
        return lax.rem(mine + 1 + k, count)
    half = count // 2
    mask, out = jnp.where(k < half, count - 1 - 2 * k, 2 * (count - 1 - k)), 0
    for i in range(count.bit_length() - 1):
        out = out + lax.rem(lax.div(mine, 1 << i) + lax.div(mask, 1 << i), 2) * (1 << i)
    return out


def take(row, lane):
    return jnp.take_along_axis(row, lane, axis=1, mode="promise_in_bounds")


def kernel(n, m, vol_hbm, idx_hbm, table_hbm, out, vol, idx, table, load_sem, fvol, weight, across, slope, square, base, depths,
           part, other, mix, recv, edge, from_left, from_right, zlo, zhi, halo, pair_send, pair_recv, send_sem, recv_sem, halo_send, halo_recv):
    depth, rows, cols = vol.shape
    rb = rows // n
    group = UNIT // rb
    units = rows // UNIT
    tiles = UNIT // SUB
    me = lax.axis_index("depth")
    mine = lax.axis_index("col")
    my_unit = lax.div(me, group)

    def start_of(k):
        return place_of(jnp.minimum(k, units - 1), my_unit, units) * UNIT

    def load_labels(k, start):
        at = pl.ds(pl.multiple_of(start, UNIT), UNIT)
        return pltpu.make_async_copy(idx_hbm.at[:, at], idx.at[:, at], load_sem.at[k])

    step = depth // CHUNKS
    loads = [pltpu.make_async_copy(table_hbm, table, load_sem.at[units])]
    for i in range(CHUNKS):
        at = pl.ds(i * step, step)
        loads.append(pltpu.make_async_copy(vol_hbm.at[at], vol.at[at], load_sem.at[units + 1 + i]))
    for load in loads:
        load.start()

    barrier = pltpu.get_barrier_semaphore()

    def greet(k, c):
        pl.semaphore_signal(barrier, inc=1, device_id={"depth": lax.rem(me + 1 + k, n)}, device_id_type=MESH)
        return c

    lax.fori_loop(0, n - 1, greet, 0, unroll=True)
    for there, side in ((mine > 0, -1), (mine < m - 1, 1)):
        @pl.when(there)
        def _():
            pl.semaphore_signal(barrier, inc=1, device_id={"col": mine + side}, device_id_type=MESH)

    lax.fori_loop(0, units, lambda k, c: (load_labels(k, start_of(k)).start(), c)[1], 0, unroll=True)

    def halo_copy(k, src, dst, axis, to):
        return pltpu.make_async_remote_copy(
            src_ref=src, dst_ref=dst, send_sem=halo_send.at[k], recv_sem=halo_recv.at[k],
            device_id={axis: to}, device_id_type=MESH)

    halos = ((me > 0, me < n - 1, halo_copy(0, vol.at[0], zhi, "depth", me - 1), zhi),
             (me < n - 1, me > 0, halo_copy(1, vol.at[depth - 1], zlo, "depth", me + 1), zlo),
             (mine > 0, mine < m - 1, halo_copy(2, edge, from_right, "col", mine - 1), from_right),
             (mine < m - 1, mine > 0, halo_copy(3, edge, from_left, "col", mine + 1), from_left))

    r_i = lax.broadcasted_iota(jnp.int32, (cols, cols), 0)
    c_i = lax.broadcasted_iota(jnp.int32, (cols, cols), 1)
    diff = jnp.where(r_i == c_i + 1, 1.0, 0.0) - jnp.where(r_i == c_i - 1, 1.0, 0.0)
    diff = diff.astype(jnp.bfloat16)
    zero = jnp.zeros((PAD, cols), jnp.float32)

    loads[0].wait()
    entries = table[...].astype(jnp.float32)
    sigma = entries[3:4]
    alpha = one_minus_exp(sigma)
    logs = [jnp.log(jnp.maximum(v, 1.2e-38)) * LOG2E
            for v in [entries[c:c + 1] * alpha for c in range(3)] + [sigma * LOG2E]]
    most = [jnp.max(v, axis=1, keepdims=True) for v in logs]
    least = [jnp.min(v, axis=1, keepdims=True) for v in logs]
    middle = [0.5 * (a + b) for a, b in zip(most, least)]
    grain = [jnp.maximum(a - b, 1e-3) * (1.0 / 65532.0) for a, b in zip(most, least)]
    place = [(v - o) / g for v, o, g in zip(logs, middle, grain)]

    def word(upper, lower):
        lower = jnp.floor(lower + 0.5)
        upper = jnp.floor(upper - lower * (1.0 / 65536.0) + 0.5)
        return upper.astype(jnp.int32) * 65536 + lower.astype(jnp.int32)

    words = (word(place[0], place[1]), word(place[2], place[3]))
    low = [jnp.broadcast_to(t[:, :128], (SUB, 128)) for t in words]
    high = [jnp.broadcast_to(t[:, 128:], (SUB, 128)) for t in words]
    spread = [jnp.broadcast_to(g * (1.0 / 65536.0), (SUB, cols)) for g in grain]
    sigma_middle = jnp.broadcast_to(middle[3], (SUB, cols))
    scale = [jnp.broadcast_to(jnp.exp2(o), (SUB, cols)) for o in middle[:3]]

    def widen(z, c):
        fvol[z + 1, :PAD] = zero
        fvol[z + 1, PAD + rows:] = zero
        fvol[z + 1, PAD:PAD + rows] = vol[z].astype(jnp.float32)
        return c

    for i in range(CHUNKS):
        loads[1 + i].wait()
        lax.fori_loop(i * step, (i + 1) * step, widen, 0)

    def pick(z, total):
        at = jnp.where((r_i == cols - 1) & (c_i == z), 1.0, 0.0)
        at = at + jnp.where((r_i == 0) & (c_i == depth + z), 1.0, 0.0)
        return total + jnp.dot(vol[z], at.astype(jnp.bfloat16), preferred_element_type=jnp.float32)

    fold = cols // (2 * depth)
    short = rows // fold

    def pack_edges():
        edges = lax.fori_loop(0, depth, pick, jnp.zeros((rows, cols), jnp.float32), unroll=True)
        packed = edges[:short]
        for i in range(1, fold):
            packed = packed + pltpu.roll(edges[i * short:(i + 1) * short], 2 * depth * i, 1)
        edge[...] = packed.astype(jnp.bfloat16)

    def look(k, start):
        @pl.when(k == 1)
        def _():
            pack_edges()
            neighbours = (mine > 0).astype(jnp.int32) + (mine < m - 1).astype(jnp.int32)
            pl.semaphore_wait(barrier, n - 1 + neighbours)
            for sends, _, copy, _ in halos:
                pl.when(sends)(copy.start)

        load_labels(k, start).wait()
        u0 = pl.multiple_of(start, UNIT)
        sums = [[jnp.zeros((SUB, cols), jnp.float32) for _ in range(4)] for _ in range(tiles)]
        def decode(z, i, first, second, gxs):
            r = slice(i * SUB, (i + 1) * SUB)
            acc0, acc1, acc2, s = sums[i]
            codes = (first, first << 16, second, second << 16)
            code0, code1, code2, code3 = [v.astype(jnp.float32) * g for v, g in zip(codes, spread)]
            w0, w1, w2 = jnp.exp2(code0 + s), jnp.exp2(code1 + s), jnp.exp2(code2 + s)
            weight[k, 0, z, r], weight[k, 1, z, r], weight[k, 2, z, r] = w0, w1, w2
            sums[i] = [acc0 + w0, acc1 + w1, acc2 + w2, s - jnp.exp2(code3 + sigma_middle)]
            at = pl.multiple_of(PAD + u0 + i * SUB, SUB)
            gy = fvol[z + 1, pl.ds(at + 1, SUB)] - fvol[z + 1, pl.ds(at - 1, SUB)]
            facing = gy * LIGHT[1]
            norm = gy * gy + 4.0
            if 0 < z < depth - 1:
                gz = fvol[z + 2, pl.ds(at, SUB)] - fvol[z, pl.ds(at, SUB)]
                facing = facing + gz * LIGHT[2]
                norm = norm + gz * gz
            across[k, z, r] = gxs[r]
            slope[k, z, r] = facing
            square[k, z, r] = norm

        places = [(z, i) for z in range(depth) for i in range(tiles)]
        gx = [jnp.dot(vol[z, pl.ds(u0, UNIT)], diff, preferred_element_type=jnp.float32) for z in range(depth)]
        got, busy, open_at = {}, [3, 0], [None, None]
        fresh = iter(places)
        decoded = 0
        while decoded < len(places):
            side = 1 if busy[1] <= busy[0] else 0
            if open_at[side] is None:
                place = next(fresh, None)
                if place is None:
                    side = 1 - side
                    if open_at[side] is None:
                        break
                else:
                    z, i = place
                    label = idx[z, pl.ds(u0 + i * SUB, SUB)]
                    open_at[side] = (place, label & 127, label < 128, [])
                    busy[side] += 1 - side
            place, lane, lower, words = open_at[side]
            words.append(take((low[1], high[1], low[0], high[0])[len(words)], lane))
            busy[side] += 1
            if len(words) == 4:
                got[place] = jnp.where(lower, words[2], words[3]), jnp.where(lower, words[0], words[1])
                open_at[side] = None
            while decoded < len(places) and places[decoded] in got:
                z, i = places[decoded]
                decode(z, i, *got[z, i], gx[z])
                decoded += 1
        for i in range(tiles):
            r = slice(i * SUB, (i + 1) * SUB)
            for c3 in range(3):
                base[k, c3, r] = sums[i][c3] * 0.25
            depths[k, r] = sums[i][3]
        return start_of(k + 1)

    lax.fori_loop(0, units, look, start_of(0))

    for sends, receives, copy, landed in halos:
        pl.when(sends)(copy.wait_send)
        pl.when(receives)(copy.wait_recv)

        @pl.when(jnp.logical_not(receives))
        def _():
            landed[...] = jnp.zeros_like(landed)

    fvol[0, PAD:PAD + rows] = zlo[...].astype(jnp.float32)
    fvol[depth + 1, PAD:PAD + rows] = zhi[...].astype(jnp.float32)
    lane = lax.broadcasted_iota(jnp.int32, (short, cols), 1)
    packed = jnp.where(lax.rem(lane, 2 * depth) < depth, -from_left[...].astype(jnp.float32),
                       from_right[...].astype(jnp.float32))
    for i in range(fold):
        mine_here = pltpu.roll(packed, cols - 2 * depth * i, 1) if i else packed
        halo[i * short:(i + 1) * short] = jnp.where(lane < 2 * depth, mine_here, 0.0)
    lane = lax.broadcasted_iota(jnp.int32, (SUB, cols), 1)

    odd = lax.rem(me, 2)
    partner = me + 1 - 2 * odd
    behind = odd.astype(jnp.float32)
    pairs = n // 2
    my_pair = lax.div(me, 2)

    def block_of(k, j):
        return place_of(k, my_unit, units) * group + j

    def hand_over(k, j):
        slot = lax.div(block_of(k, j), 2)
        return pltpu.make_async_remote_copy(
            src_ref=part.at[k, j], dst_ref=other.at[slot], send_sem=pair_send.at[slot], recv_sem=pair_recv.at[slot],
            device_id={"depth": partner}, device_id_type=MESH)

    def deliver(to):
        slot = lax.div(to, 2)
        return pltpu.make_async_remote_copy(
            src_ref=mix.at[slot], dst_ref=recv.at[my_pair], send_sem=send_sem.at[slot], recv_sem=recv_sem.at[my_pair],
            device_id={"depth": to}, device_id_type=MESH)

    def merge(k, j, own):
        to = block_of(k, j)
        slot = lax.div(to, 2)
        hand_over(k, j).wait_recv()
        theirs = [other[slot, c * rb:(c + 1) * rb] for c in range(4)]
        front = jnp.exp2(theirs[3] * behind)
        back = jnp.exp2(own[3] * (1.0 - behind))
        both = [own[c] * front + theirs[c] * back for c in range(3)] + [own[3] + theirs[3]]
        both = jnp.concatenate(both, 0).astype(jnp.bfloat16)

        @pl.when(to != me)
        def _():
            mix[slot] = both
            deliver(to).start()

        @pl.when(to == me)
        def _():
            recv[my_pair] = both

    def shade(k, start):
        u0 = pl.multiple_of(start, UNIT)
        sums = [[base[k, c3, i * SUB:(i + 1) * SUB] for c3 in range(3)] for i in range(tiles)]
        ends = [halo[pl.ds(u0 + i * SUB, SUB)] for i in range(tiles)]
        for z in range(depth):
            outer = jnp.where(lane == 0, z, jnp.where(lane == cols - 1, depth + z, cols - 1))
            for i in range(tiles):
                r = slice(i * SUB, (i + 1) * SUB)
                gx = across[k, z, r] + take(ends[i], outer)
                facing = slope[k, z, r] + gx * LIGHT[0]
                norm = square[k, z, r] + gx * gx
                if z == 0 or z == depth - 1:
                    at = pl.multiple_of(PAD + u0 + i * SUB, SUB)
                    gz = fvol[z + 2, pl.ds(at, SUB)] - fvol[z, pl.ds(at, SUB)]
                    facing = facing + gz * LIGHT[2]
                    norm = norm + gz * gz
                lit = jnp.abs(facing) * lax.rsqrt(norm)
                sums[i] = [a + weight[k, c3, z, r] * lit for c3, a in enumerate(sums[i])]
        color = [jnp.concatenate([sums[i][c3] * scale[c3] for i in range(tiles)], 0) for c3 in range(3)]
        return color + [depths[k]]

    def give(k, start):
        color = shade(k, start)
        for j in range(group):
            part[k, j] = jnp.concatenate([v[j * rb:(j + 1) * rb] for v in color], 0)
            if paired:
                hand_over(k, j).start()
            else:
                pl.when(lax.rem(block_of(k, j) + me, 2) == 1)(hand_over(k, j).start)
        return start_of(k + 1)

    def keep(k, start):
        merge(k, 0, shade(k, start))
        return start_of(k + 1)

    def gather_pair(k, c):
        for j in range(group):
            @pl.when(lax.rem(block_of(k, j) + me, 2) == 0)
            def _():
                merge(k, j, [part[k, j, c3 * rb:(c3 + 1) * rb] for c3 in range(4)])
        return c

    paired = group == 1 and units & (units - 1) == 0
    if paired:
        start = lax.fori_loop(0, units // 2, give, start_of(0))
        lax.fori_loop(units // 2, units, keep, start)
    else:
        lax.fori_loop(0, units, give, start_of(0))
        lax.fori_loop(0, units, gather_pair, 0)

    def arrive(k, c):
        @pl.when(k != my_pair)
        def _():
            pltpu.make_async_remote_copy(
                src_ref=mix.at[0], dst_ref=recv.at[k], send_sem=send_sem.at[0], recv_sem=recv_sem.at[k],
                device_id={"depth": 2 * k + odd}, device_id_type=MESH).wait_recv()
        return c

    lax.fori_loop(0, pairs, arrive, 0)

    def over(j, carry):
        color, s = carry
        piece = recv[j].astype(jnp.float32)
        t = jnp.exp2(s)
        color = tuple(color[c] + t * piece[c * rb:(c + 1) * rb] for c in range(3))
        return color, s + piece[3 * rb:]

    init = jnp.zeros((rb, cols), jnp.float32)
    color, s = lax.fori_loop(0, pairs, over, ((init,) * 3, init), unroll=4)
    for c in range(3):
        out[c] = color[c]
    out[3] = one_minus_exp(s * -LN2)

    def left(slot, c):
        pltpu.make_async_remote_copy(
            src_ref=part.at[0, 0], dst_ref=other.at[slot], send_sem=pair_send.at[slot], recv_sem=pair_recv.at[slot],
            device_id={"depth": partner}, device_id_type=MESH).wait_send()

        @pl.when(slot != my_pair)
        def _():
            deliver(2 * slot + odd).wait_send()
        return c

    lax.fori_loop(0, pairs, left, 0)


def on_device(volume, tf_index, tf_table):
    depth, rows, cols = volume.shape
    n = lax.axis_size("depth")
    m = lax.axis_size("col")
    vm = pl.BlockSpec(memory_space=pltpu.VMEM)
    rb = rows // n
    units, group = rows // UNIT, UNIT // rb
    return pl.pallas_call(
        functools.partial(kernel, n, m),
        out_shape=jax.ShapeDtypeStruct((4, rb, cols), jnp.float32),
        in_specs=[pl.BlockSpec(memory_space=pltpu.HBM)] * 3,
        out_specs=vm,
        scratch_shapes=[
            pltpu.VMEM(volume.shape, volume.dtype),
            pltpu.VMEM(tf_index.shape, tf_index.dtype),
            pltpu.VMEM(tf_table.shape, tf_table.dtype),
            pltpu.SemaphoreType.DMA((units + 1 + CHUNKS,)),
            pltpu.VMEM((depth + 2, rows + 2 * PAD, cols), jnp.float32),
            pltpu.VMEM((units, 3, depth, UNIT, cols), jnp.float32),
            *[pltpu.VMEM((units, depth, UNIT, cols), jnp.float32)] * 3,
            pltpu.VMEM((units, 3, UNIT, cols), jnp.float32),
            pltpu.VMEM((units, UNIT, cols), jnp.float32),
            pltpu.VMEM((units, group, 4 * rb, cols), jnp.float32),
            pltpu.VMEM((n // 2, 4 * rb, cols), jnp.float32),
            *[pltpu.VMEM((n // 2, 4 * rb, cols), jnp.bfloat16)] * 2,
            *[pltpu.VMEM((2 * rows * depth // cols, cols), jnp.bfloat16)] * 3,
            *[pltpu.VMEM((rows, cols), jnp.bfloat16)] * 2,
            pltpu.VMEM((rows, cols), jnp.float32),
            *[pltpu.SemaphoreType.DMA((n // 2,))] * 4,
            pltpu.SemaphoreType.DMA((4,)),
            pltpu.SemaphoreType.DMA((4,)),
        ],
        compiler_params=pltpu.CompilerParams(
            collective_id=0, has_side_effects=True, vmem_limit_bytes=53 * 1024 * 1024),
    )(volume, tf_index, tf_table)


def solution(mesh):
    in_specs = (P("depth", None, "col"), P("depth", None, "col"), P())
    out_specs = P(None, "depth", "col")
    return jax.shard_map(
        on_device, mesh=mesh, in_specs=in_specs, out_specs=out_specs, check_vma=False
    )
```
